32 devices in a mesh: groups: 2 (over y), adapter: 4 (over z), head: 4 (over x, core).
Axes of the slice: x: 2, y: 2, z: 4, core: 2. Of those that a mesh axis runs over, the one named last changes fastest.
Arguments:
- normed_hidden_rows: bfloat16 [256, 8192], P(('groups', 'adapter'), 'head'), parts along dimension 0, may hold values from -6 to 6
- base_query: bfloat16 [256, 8192], P(('groups', 'adapter'), 'head'), parts along dimension 0, may hold values from -6 to 6
- base_key_value: bfloat16 [256, 2, 1024], P(('groups', 'adapter'), None, 'head'), parts along dimension 0, may hold values from -6 to 6
- key_value_cache: bfloat16 [2560, 2, 16, 1024], P(('groups', 'adapter'), None, None, 'head'), parts along dimension 0, may hold values from -6 to 6
- cached_length_per_request: int32 [256], P(('groups', 'adapter')), parts along dimension 0, may hold values from 1 to 2560, as said below
- request_page_table: int32 [256, 160], P(('groups', 'adapter')), parts along dimension 0, may hold values from 0 to 319, as said below
- planned_request_rows: int32 [256], P('groups'), parts along dimension 0, may hold values from 0 to 127, as said below
- request_adapters: int32 [256], P('groups'), parts along dimension 0, may hold values from 0 to 15, as said below
- query_key_value_down_maps: bfloat16 [16, 8192, 96], P('adapter', 'head'), may hold values from -0.0625 to 0.0625
- query_up_maps: bfloat16 [16, 32, 8192], P('adapter', None, 'head'), may hold values from -1 to 1
- key_value_up_maps: bfloat16 [16, 2, 32, 1024], P('adapter', None, None, 'head'), may hold values from -1 to 1
- output_down_maps: bfloat16 [16, 8192, 32], P('adapter', 'head'), may hold values from -0.25 to 0.25
- output_up_maps: bfloat16 [16, 32, 8192], P('adapter', 'head'), may hold values from -1 to 1
- output_weight_matrix: bfloat16 [8192, 8192], P('head', 'adapter'), may hold values from -0.25 to 0.25
Outputs:
- block_out: bfloat16 [256, 8192], P(('groups', 'head'), 'adapter'), parts along dimension 0
The draws below stay inside these ranges and needn't reach their ends.
There are 2 independent parts, one for each index of `groups`. The reference program is written for one: setup_inputs(seed, part) draws one part's arguments, and reference() takes and returns one part's arrays. A program takes and returns all parts, laid end to end along the dimension named above; an argument that names none is the same for every part. Nothing has to cross between parts.
Inputs may be any that keep to these rules, and one draw needn't show every extreme that they name: `planned_request_rows`: A permutation. Planned rows k * 32 to (k + 1) * 32 - 1 are the requests of home k. `request_adapters`: adapter i is owned by index i // 4 of adapter. Among the 32 planned rows of one home, at most 16 use adapters of any one owner; in every draw one owner takes exactly 16 rows from every home. `cached_length_per_request`: on each home the requests need ceil(length / 16) pages each and at most 320 in all; one request of each home holds exactly 2560 tokens. `request_page_table`: entries index the pool of the request's home. The 160 entries of a row are distinct; the first ceil(length / 16) of them are pages of that request alone, the rest are other pages of the same pool.
All inputs are finite; a program needn't handle non-finite values.
Results may differ from the reference program's by a relative error of at most 0.0075.
Values may be sent and summed in bfloat16 or wider, within the bound.
A program may use at most 128 MiB of HBM per device.

```python
import jax
import jax.numpy as jnp
from jax import lax

MODEL_WIDTH = 8192
QH = 64
KVH = 8
HD = 128
ADAPTER_RANK = 32
ADP_DEV = 4
PAGE = 16
PAGES_DEV = 320
MAXP = 160
REQ_DEV = 32
HOMES = 4
REQUESTS = 128
ADAPTER_TOTAL = 16
QUERY_WIDTH = 8192
KEY_VALUE_WIDTH = 1024
SLOT = 16


def _plan(key):
    split_keys = jax.random.split(key, 11)
    forced = jax.random.randint(split_keys[0], (), 0, HOMES)
    popular = jax.random.randint(split_keys[1], (HOMES,), 0, 3)
    jitter = jax.random.randint(split_keys[2], (HOMES, HOMES, SLOT), 0, 4096)
    popularity_boost = jax.random.randint(split_keys[3], (HOMES, HOMES, SLOT), 0, 4096) * popular[None, :, None]
    owner_axis = jnp.arange(HOMES, dtype=jnp.int32)[None, :, None]
    owner_score = jitter + popularity_boost + jnp.where(owner_axis == forced, 16384, 0)
    flat_score = owner_score.reshape(HOMES, HOMES * SLOT) * (HOMES * SLOT) + jnp.arange(HOMES * SLOT, dtype=jnp.int32)[None, :]
    top_values, chosen = lax.top_k(flat_score, REQ_DEV)
    owners = chosen // SLOT
    shuffle = jax.random.randint(split_keys[4], (HOMES, REQ_DEV), 0, 65536) * REQ_DEV + jnp.arange(REQ_DEV, dtype=jnp.int32)[None, :]
    row_order = jnp.argsort(shuffle, axis=1)
    owners = jnp.take_along_axis(owners, row_order, axis=1)
    local_index = jax.random.randint(split_keys[5], (HOMES, REQ_DEV), 0, ADP_DEV)
    planned = (owners * ADP_DEV + local_index).reshape(REQUESTS).astype(jnp.int32)
    planned_request_rows = jax.random.permutation(split_keys[6], REQUESTS).astype(jnp.int32)
    request_adapters = jnp.zeros((REQUESTS,), jnp.int32).at[planned_request_rows].set(planned)
    weights = jax.random.randint(split_keys[7], (HOMES, REQ_DEV), 1, 9)
    longest = jax.random.randint(split_keys[8], (HOMES,), 0, REQ_DEV)
    is_longest = jnp.arange(REQ_DEV, dtype=jnp.int32)[None, :] == longest[:, None]
    spare_pages = PAGES_DEV - MAXP - (REQ_DEV - 1)
    others_weight = jnp.where(is_longest, 0, weights)
    weight_sum = jnp.sum(others_weight, axis=1, keepdims=True)
    page_counts = jnp.where(is_longest, MAXP, 1 + others_weight * spare_pages // weight_sum)
    last_page_fill = jax.random.randint(split_keys[9], (HOMES, REQ_DEV), 1, PAGE + 1)
    lengths = jnp.where(is_longest, MAXP * PAGE, (page_counts - 1) * PAGE + last_page_fill)
    pool_score = jax.random.randint(split_keys[10], (HOMES, PAGES_DEV), 0, 65536) * PAGES_DEV + jnp.arange(PAGES_DEV, dtype=jnp.int32)[None, :]
    pool_order = jnp.argsort(pool_score, axis=1).astype(jnp.int32)
    starts = jnp.cumsum(page_counts, axis=1) - page_counts
    entry_index = (starts[:, :, None] + jnp.arange(MAXP, dtype=jnp.int32)[None, None, :]) % PAGES_DEV
    page_rows = jax.vmap(lambda order_row, entry_row: order_row[entry_row])(pool_order, entry_index)
    return (planned_request_rows, request_adapters, lengths.reshape(REQUESTS).astype(jnp.int32), page_rows.reshape(REQUESTS, MAXP).astype(jnp.int32))


def draw_planned_request_rows(key, part):
    return _plan(key)[0]


def draw_request_adapters(key, part):
    return _plan(key)[1]


def draw_cached_length_per_request(key, part):
    return _plan(key)[2]


def draw_request_page_table(key, part):
    return _plan(key)[3]


def draw_base_query(key, part):
    key = jax.random.fold_in(key, 21)
    values = jnp.clip(jax.random.normal(key, (REQUESTS, QH, HD), jnp.float32), -6.0, 6.0)
    return values.reshape(REQUESTS, QUERY_WIDTH).astype(jnp.bfloat16)


def draw_key_value_cache(key, part):
    key = jax.random.fold_in(key, 22)
    first_key = jax.random.fold_in(key, 0)
    cache_shape = (HOMES * PAGES_DEV, 2, PAGE, KVH, HD)
    values = jnp.clip(jax.random.normal(first_key, cache_shape, jnp.float32), -6.0, 6.0)
    return values.reshape(HOMES * PAGES_DEV, 2, PAGE, KEY_VALUE_WIDTH).astype(jnp.bfloat16)


def block_levels(stream_key, extent, cuts, least, largest):
    level = 1.0
    for position, blocks in cuts:
        heights = jax.random.uniform(jax.random.fold_in(jax.random.fold_in(stream_key, 6), position), (blocks,), jnp.float32, least / len(cuts), largest / len(cuts))
        level = level * jnp.repeat(jnp.exp(heights), extent[position] // blocks).reshape((-1,) + (1,) * (len(extent) - 1 - position))
    return level


def noise(own_key, extent, width, limit, pieces=(), kind=jnp.bfloat16):
    values = width * jax.random.normal(own_key, extent, jnp.float32)
    if pieces:
        values = values * block_levels(own_key, extent, pieces, -0.22, 0.18)
    return jnp.clip(values, -limit, limit).astype(kind)


def setup_inputs(seed: int = 0, part: int = 0) -> dict:
    splits = jax.random.split(jax.random.key(seed), 15)
    part_keys = jax.random.split(jax.random.fold_in(splits[14], part), 15)
    return {
        "normed_hidden_rows": noise(part_keys[0], (REQUESTS, MODEL_WIDTH), 1.0, 6.0, ((0, 4), (1, 4))),
        "base_query": draw_base_query(jax.random.fold_in(jax.random.fold_in(splits[14], part), 71), part),
        "base_key_value": noise(part_keys[2], (REQUESTS, 2, KEY_VALUE_WIDTH), 1.0, 6.0, ((0, 4), (2, 4))),
        "key_value_cache": draw_key_value_cache(jax.random.fold_in(jax.random.fold_in(splits[14], part), 71), part),
        "cached_length_per_request": draw_cached_length_per_request(jax.random.fold_in(jax.random.fold_in(splits[14], part), 71), part),
        "request_page_table": draw_request_page_table(jax.random.fold_in(jax.random.fold_in(splits[14], part), 71), part),
        "planned_request_rows": draw_planned_request_rows(jax.random.fold_in(jax.random.fold_in(splits[14], part), 71), part),
        "request_adapters": draw_request_adapters(jax.random.fold_in(jax.random.fold_in(splits[14], part), 71), part),
        "query_key_value_down_maps": noise(splits[8], (ADAPTER_TOTAL, MODEL_WIDTH, 3 * ADAPTER_RANK), MODEL_WIDTH ** -0.5, 0.0625, ((0, 4), (1, 4))),
        "query_up_maps": noise(splits[9], (ADAPTER_TOTAL, ADAPTER_RANK, QUERY_WIDTH), ADAPTER_RANK ** -0.5, 1.0, ((0, 4), (2, 4))),
        "key_value_up_maps": noise(splits[10], (ADAPTER_TOTAL, 2, ADAPTER_RANK, KEY_VALUE_WIDTH), ADAPTER_RANK ** -0.5, 1.0, ((0, 4), (3, 4))),
        "output_down_maps": noise(splits[11], (ADAPTER_TOTAL, QUERY_WIDTH, ADAPTER_RANK), (QUERY_WIDTH // 16) ** -0.5, 0.25, ((0, 4), (1, 4))),
        "output_up_maps": noise(splits[12], (ADAPTER_TOTAL, ADAPTER_RANK, MODEL_WIDTH), ADAPTER_RANK ** -0.5, 1.0, ((0, 4), (1, 4))),
        "output_weight_matrix": noise(splits[13], (QUERY_WIDTH, MODEL_WIDTH), (QUERY_WIDTH // 16) ** -0.5, 0.25, ((0, 4), (1, 4))),
    }


def reference(normed_hidden_rows, base_query, base_key_value, key_value_cache, cached_length_per_request, request_page_table, planned_request_rows, request_adapters, query_key_value_down_maps, query_up_maps, key_value_up_maps, output_down_maps, output_up_maps, output_weight_matrix):
    row_adapters = request_adapters[planned_request_rows].astype(jnp.int32)
    group_size = QH // KVH
    score_scale = HD ** -0.5

    def adapt_in(item):
        hidden_state_row, adapter_for_row = item
        reduced_rows = jnp.dot(hidden_state_row, query_key_value_down_maps[adapter_for_row], preferred_element_type=jnp.float32).astype(jnp.bfloat16)
        query_up_delta = jnp.dot(reduced_rows[:ADAPTER_RANK], query_up_maps[adapter_for_row], preferred_element_type=jnp.float32)
        key_up_delta = jnp.dot(reduced_rows[ADAPTER_RANK:2 * ADAPTER_RANK], key_value_up_maps[adapter_for_row, 0], preferred_element_type=jnp.float32)
        value_up_delta = jnp.dot(reduced_rows[2 * ADAPTER_RANK:], key_value_up_maps[adapter_for_row, 1], preferred_element_type=jnp.float32)
        return (0.5 * jnp.concatenate([query_up_delta, key_up_delta, value_up_delta])).astype(jnp.bfloat16)

    delta_qkv = lax.map(adapt_in, (normed_hidden_rows, row_adapters))
    delta_wide = delta_qkv.astype(jnp.float32)
    query_rows = (base_query.astype(jnp.float32) + delta_wide[:, :QUERY_WIDTH]).astype(jnp.bfloat16)
    key_new = (base_key_value[:, 0].astype(jnp.float32) + delta_wide[:, QUERY_WIDTH:QUERY_WIDTH + KEY_VALUE_WIDTH]).astype(jnp.bfloat16)
    value_new = (base_key_value[:, 1].astype(jnp.float32) + delta_wide[:, QUERY_WIDTH + KEY_VALUE_WIDTH:]).astype(jnp.bfloat16)

    homes_of = jnp.arange(REQUESTS, dtype=jnp.int32) // REQ_DEV
    global_pages = (request_page_table + (homes_of * PAGES_DEV)[:, None]).astype(jnp.int32)

    def attend(item):
        query_row, key_row, value_row, pages, length = item
        gathered = key_value_cache[pages]
        cached_keys = gathered[:, 0].reshape(MAXP * PAGE, KVH, HD).astype(jnp.float32)
        cached_values = gathered[:, 1].reshape(MAXP * PAGE, KVH, HD).astype(jnp.float32)
        heads = query_row.reshape(KVH, group_size, HD).astype(jnp.float32)
        scores = jnp.einsum("kgd,tkd->kgt", heads, cached_keys) * score_scale
        own_score = jnp.einsum("kgd,kd->kg", heads, key_row.reshape(KVH, HD).astype(jnp.float32)) * score_scale
        valid = jnp.arange(MAXP * PAGE, dtype=jnp.int32) < length
        scores = jnp.where(valid[None, None, :], scores, -jnp.inf)
        row_top = jnp.maximum(jnp.max(scores, axis=2), own_score)
        weights = jnp.exp(scores - row_top[:, :, None])
        own_weight = jnp.exp(own_score - row_top)
        weight_sum = jnp.sum(weights, axis=2) + own_weight
        probabilities = (weights / weight_sum[:, :, None]).astype(jnp.bfloat16)
        own_probability = (own_weight / weight_sum).astype(jnp.bfloat16)
        mixed_heads = jnp.einsum("kgt,tkd->kgd", probabilities.astype(jnp.float32), cached_values)
        mixed_heads = mixed_heads + own_probability.astype(jnp.float32)[:, :, None] * value_row.reshape(KVH, 1, HD).astype(jnp.float32)
        return mixed_heads.reshape(QUERY_WIDTH).astype(jnp.bfloat16)

    attended = lax.map(attend, (query_rows, key_new, value_new, global_pages, cached_length_per_request))
    base_out = jnp.dot(attended, output_weight_matrix, preferred_element_type=jnp.float32)

    def adapt_out(item):
        attention_result_row, adapter_for_row = item
        reduced_rows = jnp.dot(attention_result_row, output_down_maps[adapter_for_row], preferred_element_type=jnp.float32).astype(jnp.bfloat16)
        return 0.5 * jnp.dot(reduced_rows, output_up_maps[adapter_for_row], preferred_element_type=jnp.float32)

    delta_o = lax.map(adapt_out, (attended, row_adapters))
    return (base_out + delta_o).astype(jnp.bfloat16)
```

```python
import functools
import math

import jax
import jax.numpy as jnp
from jax import lax
from jax.experimental import pallas as pl
from jax.experimental.pallas import tpu as pltpu
from jax.sharding import PartitionSpec as P

QH = 64
KVH = 8
HD = 128
BF = jnp.bfloat16
F32 = jnp.float32
I32 = jnp.int32
CHUNK_PAGES = 64


def iota(shape, dim):
    return lax.broadcasted_iota(I32, shape, dim)


def mm(a, b, dims=((1,), (0,))):
    return lax.dot_general(a, b, (dims, ((), ())), preferred_element_type=F32)


def kernel(
    cfg,
    hid_ref, bq_ref, bkv_ref, len_ref, table_ref, plan_ref, reqad_ref,
    cache_hbm, down_hbm, qup_hbm, kvup_hbm, odown_hbm, oup_hbm, w_hbm,
    out_ref,
    cache_v, down_v, qup_v, kvup_v, odown_v, w_v,
    row_out, row_in, ps_out, ps_in, dl_out, dl_in, up_all, odc,
    bias_s, score_s, att, tot, rr_out, rr_in, ag, fin_out, fin_in,
    lsem, row_ss, row_rs, ps_ss, ps_rs, dl_ss, dl_rs, up_ss, up_rs,
    att_ss, att_rs, rr_ss, rr_rs, ag_ss, ag_rs, fin_ss, fin_rs,
):
    n, nh, rows, slot, na, rank = cfg
    total = n * rows
    cells = n * slot
    group = QH // KVH
    kvl = bkv_ref.shape[2] // HD
    half = group * HD
    qw = kvl * half
    kvw = kvl * HD
    z = lax.axis_index("adapter")
    h = lax.axis_index("head")

    def peer_z(d):
        return lax.rem(z + d, n)

    def peer_h(d):
        return lax.rem(h + d, nh)

    def rcopy(src, dst, ss, rs, axis, dev):
        return pltpu.make_async_remote_copy(
            src_ref=src, dst_ref=dst, send_sem=ss, recv_sem=rs,
            device_id={axis: dev}, device_id_type=pl.DeviceIdType.MESH,
        )

    locals_ = []
    for i, (src, dst) in enumerate((
        (down_hbm, down_v), (qup_hbm, qup_v), (kvup_hbm, kvup_v),
        (cache_hbm, cache_v), (odown_hbm, odown_v), (w_hbm, w_v),
    )):
        cp = pltpu.make_async_copy(src, dst, lsem.at[i])
        cp.start()
        locals_.append(cp)
    own_up = pltpu.make_async_copy(
        oup_hbm.at[:, pl.ds(pl.multiple_of(z * w_v.shape[1], 128), w_v.shape[1])],
        up_all.at[z], lsem.at[6])
    own_up.start()

    barrier = pltpu.get_barrier_semaphore()
    for d in range(1, n):
        pl.semaphore_signal(barrier, inc=1, device_id={"adapter": peer_z(d)},
                            device_id_type=pl.DeviceIdType.MESH)
    for d in range(1, nh):
        pl.semaphore_signal(barrier, inc=1, device_id={"head": peer_h(d)},
                            device_id_type=pl.DeviceIdType.MESH)

    jj = iota((total, total), 0)
    ii = iota((total, total), 1)
    eye = jj == ii

    def to_col(row):
        return jnp.sum(jnp.where(eye, row, 0), axis=1, keepdims=True)

    def to_row(col):
        return jnp.sum(jnp.where(eye, col, 0), axis=0, keepdims=True)

    plan_col = to_col(plan_ref[...])
    ad_col = jnp.sum(jnp.where(plan_col == ii, reqad_ref[...], 0), axis=1, keepdims=True)
    ad_row = to_row(ad_col)
    own_col = ad_col // na
    own_row = ad_row // na
    before = (own_col == own_row) & (jj // rows == ii // rows) & (ii < jj)
    slot_col = jnp.sum(before.astype(I32), axis=1, keepdims=True)
    slot_row = to_row(slot_col)
    target_col = own_col * slot + slot_col
    mine = iota((total, rows), 0) == z * rows + iota((total, rows), 1)
    my_target = jnp.sum(jnp.where(mine, target_col, 0), axis=0, keepdims=True)
    give = (my_target == iota((cells, rows), 0)).astype(F32).astype(BF)
    place_row = (iota((1, total), 1) // rows) * slot + slot_row
    cell_hit = (own_row == z) & (place_row == iota((cells, total), 0))
    local_ad = jnp.sum(jnp.where(cell_hit, ad_row - own_row * na + 1, 0), axis=1, keepdims=True) - 1

    outgoing = mm(give, hid_ref[...]).astype(BF)
    row_out[...] = outgoing.reshape(row_out.shape)
    row_in[z] = row_out[z]

    pl.semaphore_wait(barrier, n - 1 + nh - 1)

    sends = []
    for d in range(1, n):
        o = peer_z(d)
        cp = rcopy(row_out.at[o], row_in.at[z], row_ss.at[o], row_rs.at[z], "adapter", o)
        cp.start()
        sends.append(cp)

    pages = cache_v.shape[0]
    page_len = cache_v.shape[2]
    ct = CHUNK_PAGES * page_len
    nchunk = pages // CHUNK_PAGES
    table = table_ref[...]
    page_ids = iota((rows, pages), 1)
    pos = jnp.zeros((rows, pages), I32)
    for t in range(table.shape[1]):
        pos = jnp.where(table[:, t:t + 1] == page_ids, t + 1, pos)
    len_col = jnp.sum(jnp.where(iota((rows, rows), 0) == iota((rows, rows), 1), len_ref[...], 0),
                      axis=1, keepdims=True)
    lim = jnp.where(pos > 0, jnp.clip(len_col - page_len * (pos - 1), 0, page_len), 0)
    lim = lim.astype(F32).astype(BF)
    spread = (iota((CHUNK_PAGES, ct), 1) // page_len == iota((CHUNK_PAGES, ct), 0)).astype(F32).astype(BF)
    within_page = lax.rem(iota((rows, ct), 1), page_len).astype(F32)
    for c in range(nchunk):
        wide = mm(lim[:, c * CHUNK_PAGES:(c + 1) * CHUNK_PAGES], spread)
        bias_s[c] = jnp.where(within_page < wide, 0.0, -jnp.inf)
    locals_[4].wait()
    for a in range(na):
        odc[:, a * rank:(a + 1) * rank] = odown_v[a]

    locals_[0].wait()
    for d in range(1, n):
        o = peer_z(d)
        rcopy(row_out.at[o], row_in.at[o], row_ss.at[o], row_rs.at[o], "adapter", o).wait_recv()

    received = row_in[...].reshape(cells, row_in.shape[2])
    part = jnp.zeros((cells, 3 * rank), F32)
    for a in range(na):
        part = jnp.where(local_ad == a, mm(received, down_v[a]), part)
    ps_out[...] = part
    for d in range(1, nh):
        p = peer_h(d)
        cp = rcopy(ps_out, ps_in.at[h], ps_ss.at[p], ps_rs.at[h], "head", p)
        cp.start()
        sends.append(cp)
    cols = w_v.shape[1]
    for d in range(1, n):
        o = peer_z(d)
        cp = rcopy(oup_hbm.at[:, pl.ds(pl.multiple_of(o * cols, 128), cols)], up_all.at[z],
                   up_ss.at[o], up_rs.at[z], "adapter", o)
        cp.start()
        sends.append(cp)
    locals_[1].wait()
    locals_[2].wait()
    for d in range(1, nh):
        p = peer_h(d)
        rcopy(ps_out, ps_in.at[p], ps_ss.at[p], ps_rs.at[p], "head", p).wait_recv()
        part = part + ps_in[p]
    part = part * 0.5

    def chosen(lo):
        piece = part[:, lo:lo + rank]
        return jnp.concatenate(
            [jnp.where(local_ad == a, piece, 0.0) for a in range(na)], axis=1).astype(BF)

    dl_out[:, :, :qw] = mm(chosen(0), qup_v[...]).astype(BF).reshape(n, slot, qw)
    for i in range(2):
        maps = jnp.concatenate([kvup_v[a, i] for a in range(na)], axis=0)
        dl_out[:, :, qw + i * kvw:qw + (i + 1) * kvw] = (
            mm(chosen((1 + i) * rank), maps).astype(BF).reshape(n, slot, kvw))
    dl_in[z] = dl_out[z]
    for d in range(1, n):
        o = peer_z(d)
        cp = rcopy(dl_out.at[o], dl_in.at[z], dl_ss.at[o], dl_rs.at[z], "adapter", o)
        cp.start()
        sends.append(cp)
    eye_r = (iota((rows, total), 0) + z * rows) == iota((rows, total), 1)
    target_row = own_row * slot + slot_row
    take_col = jnp.sum(jnp.where(eye_r, target_row, 0), axis=1, keepdims=True)
    take = (take_col == iota((rows, cells), 1)).astype(F32).astype(BF)
    locals_[3].wait()
    for d in range(1, n):
        o = peer_z(d)
        rcopy(dl_out.at[o], dl_in.at[o], dl_ss.at[o], dl_rs.at[o], "adapter", o).wait_recv()
    delta = mm(take, dl_in[...].reshape(cells, dl_in.shape[2]))
    query = (bq_ref[...].astype(F32) + delta[:, :qw]).astype(BF)
    key_new = (bkv_ref[:, 0, :].astype(F32) + delta[:, qw:qw + kvw]).astype(BF).astype(F32)
    value_new = (bkv_ref[:, 1, :].astype(F32) + delta[:, qw + kvw:]).astype(BF).astype(F32)

    scale = HD ** -0.5 * math.log2(math.e)
    gr = group * rows
    for k in range(kvl):
        lanes = slice(k * HD, (k + 1) * HD)
        qh = jnp.concatenate(
            [query[:, k * half + g * HD:k * half + (g + 1) * HD] for g in range(group)], axis=0)
        kn = jnp.concatenate([key_new[:, lanes]] * group, axis=0)
        vn = jnp.concatenate([value_new[:, lanes]] * group, axis=0)
        own = jnp.sum(qh.astype(F32) * kn, axis=1, keepdims=True) * scale

        def scores(c, top):
            keys = cache_v[pl.ds(c * CHUNK_PAGES, CHUNK_PAGES), 0, :, lanes].reshape(ct, HD)
            s = mm(qh, keys, ((1,), (1,))) * scale
            s = (s.reshape(group, rows, ct) + bias_s[c][None]).reshape(gr, ct)
            score_s[c] = s
            for i in range(ct // HD):
                top = jnp.maximum(top, s[:, i * HD:(i + 1) * HD])
            return top

        top = lax.fori_loop(0, nchunk, scores, jnp.full((gr, HD), -jnp.inf, F32))
        top = jnp.maximum(jnp.max(top, axis=1, keepdims=True), own)

        def mix(c, carry):
            acc, den = carry
            w = jnp.exp2(score_s[c] - top)
            for i in range(ct // HD):
                den = den + w[:, i * HD:(i + 1) * HD]
            values = cache_v[pl.ds(c * CHUNK_PAGES, CHUNK_PAGES), 1, :, lanes].reshape(ct, HD)
            return acc + mm(w.astype(BF), values), den

        zero = jnp.zeros((gr, HD), F32)
        acc, den = lax.fori_loop(0, nchunk, mix, (zero, zero))
        own_w = jnp.exp2(own - top)
        den = jnp.sum(den, axis=1, keepdims=True) + own_w
        mixed = ((acc + own_w * vn) / den).astype(BF)
        for g in range(group):
            att[k, z, :, g * HD:(g + 1) * HD] = mixed[g * rows:(g + 1) * rows]
        for d in range(1, n):
            o = peer_z(d)
            cp = rcopy(att.at[k, z], att.at[k, z], att_ss.at[k, o], att_rs.at[k, z], "adapter", o)
            cp.start()
            sends.append(cp)

    locals_[5].wait()
    nc, _, cw = tot.shape
    racc = jnp.zeros((total, na * rank), F32)
    for k in range(kvl):
        for d in range(1, n):
            o = peer_z(d)
            rcopy(att.at[k, o], att.at[k, o], att_ss.at[k, o], att_rs.at[k, o], "adapter", o).wait_recv()
        every = att[k].reshape(total, half)
        racc = racc + mm(every, odc[k * half:(k + 1) * half])
        if k == kvl - 1:
            turned = racc.T
            turned = jnp.where(ad_row == z * na + iota((na * rank, total), 0) // rank, turned, 0.0)
            ranks = turned[:rank]
            for a in range(1, na):
                ranks = ranks + turned[a * rank:(a + 1) * rank]
            rl = rank // nh
            for p in range(nh):
                rr_out[p] = ranks[p * rl:(p + 1) * rl]
            for d in range(1, nh):
                p = peer_h(d)
                cp = rcopy(rr_out.at[p], rr_in.at[h], rr_ss.at[p], rr_rs.at[h], "head", p)
                cp.start()
                sends.append(cp)
        for c in range(nc):
            term = mm(every, w_v[k * half:(k + 1) * half, c * cw:(c + 1) * cw])
            if k == 0:
                tot[c] = term
            else:
                tot[c] = tot[c] + term
            if k == kvl - 1 and c == 0:
                summed = rr_out[h]
                for d in range(1, nh):
                    p = peer_h(d)
                    rcopy(rr_out.at[p], rr_in.at[p], rr_ss.at[p], rr_rs.at[p], "head", p).wait_recv()
                    summed = summed + rr_in[p]
                ag[z] = summed
                for d in range(1, n):
                    o = peer_z(d)
                    cp = rcopy(ag.at[z], ag.at[z], ag_ss.at[o], ag_rs.at[z], "adapter", o)
                    cp.start()
                    sends.append(cp)

    for d in range(1, n):
        o = peer_z(d)
        rcopy(ag.at[o], ag.at[o], ag_ss.at[o], ag_rs.at[o], "adapter", o).wait_recv()
        rcopy(oup_hbm.at[:, pl.ds(pl.multiple_of(o * cols, 128), cols)], up_all.at[o],
              up_ss.at[o], up_rs.at[o], "adapter", o).wait_recv()
    own_up.wait()
    mine_ranks = ag[0]
    for o in range(1, n):
        mine_ranks = mine_ranks + ag[o]
    rl = rank // nh
    kk = n * na * rl
    tile = (lax.rem(iota((rl, kk), 1), rl) == iota((rl, kk), 0)).astype(F32).astype(BF)
    sel = mm(mine_ranks.astype(BF), tile, ((0,), (0,)))
    sel = jnp.where(ad_col == iota((total, kk), 1) // rl, sel * 0.5, 0.0).astype(BF)
    out_rows = total // nh
    for c in range(nc):
        ups = up_all[:, :, c * cw:(c + 1) * cw].reshape(kk, cw)
        full = tot[c] + mm(sel, ups)
        tot[c] = full
        fin_out[c] = full.astype(BF).reshape(nh, out_rows, cw)
        for d in range(1, nh):
            p = peer_h(d)
            cp = rcopy(fin_out.at[c, p], fin_in.at[c, h], fin_ss.at[c, p], fin_rs.at[c, h], "head", p)
            cp.start()
            sends.append(cp)
    for c in range(nc):
        res = tot[c, pl.ds(pl.multiple_of(h * out_rows, 8), out_rows), :]
        for d in range(1, nh):
            p = peer_h(d)
            rcopy(fin_out.at[c, p], fin_in.at[c, p], fin_ss.at[c, p], fin_rs.at[c, p], "head", p).wait_recv()
            res = res + fin_in[c, p].astype(F32)
        out_ref[:, c * cw:(c + 1) * cw] = res.astype(BF)
    for cp in sends:
        cp.wait_send()


def body(
    normed_hidden_rows,
    base_query,
    base_key_value,
    key_value_cache,
    cached_length_per_request,
    request_page_table,
    planned_request_rows,
    request_adapters,
    query_key_value_down_maps,
    query_up_maps,
    key_value_up_maps,
    output_down_maps,
    output_up_maps,
    output_weight_matrix,
):
    n = lax.axis_size("adapter")
    nh = lax.axis_size("head")
    rows, feats = normed_hidden_rows.shape
    total = planned_request_rows.shape[0]
    na, _, rank = output_down_maps.shape
    slot = max(16, 2 * rows // n)
    cells = n * slot
    qw = base_query.shape[1]
    kvw = base_key_value.shape[2]
    kvl = kvw // HD
    half = qw // kvl
    dw = qw + 2 * kvw
    cols = output_weight_matrix.shape[1]
    cw = min(512, cols)
    nc = cols // cw
    pages, _, page_len, _ = key_value_cache.shape
    ct = CHUNK_PAGES * page_len
    gr = QH // KVH * rows
    out_rows = total // nh
    rl = rank // nh
    vm = pl.BlockSpec(memory_space=pltpu.VMEM)
    hb = pl.BlockSpec(memory_space=pl.ANY)
    dma = pltpu.SemaphoreType.DMA
    ups = output_up_maps.reshape(na * output_up_maps.shape[1], -1)
    qups = query_up_maps.reshape(na * rank, qw)
    return pl.pallas_call(
        functools.partial(kernel, (n, nh, rows, slot, na, rank)),
        out_shape=jax.ShapeDtypeStruct((out_rows, cols), BF),
        in_specs=[vm] * 7 + [hb] * 7,
        out_specs=vm,
        scratch_shapes=[
            pltpu.VMEM(key_value_cache.shape, BF),
            pltpu.VMEM(query_key_value_down_maps.shape, BF),
            pltpu.VMEM(qups.shape, BF),
            pltpu.VMEM(key_value_up_maps.shape, BF),
            pltpu.VMEM(output_down_maps.shape, BF),
            pltpu.VMEM(output_weight_matrix.shape, BF),
            pltpu.VMEM((n, slot, feats), BF),
            pltpu.VMEM((n, slot, feats), BF),
            pltpu.VMEM((cells, 3 * rank), F32),
            pltpu.VMEM((nh, cells, 3 * rank), F32),
            pltpu.VMEM((n, slot, dw), BF),
            pltpu.VMEM((n, slot, dw), BF),
            pltpu.VMEM((n, ups.shape[0], cols), BF),
            pltpu.VMEM((output_down_maps.shape[1], na * rank), BF),
            pltpu.VMEM((pages // CHUNK_PAGES, rows, ct), F32),
            pltpu.VMEM((pages // CHUNK_PAGES, gr, ct), F32),
            pltpu.VMEM((kvl, n, rows, half), BF),
            pltpu.VMEM((nc, total, cw), F32),
            pltpu.VMEM((nh, rl, total), F32),
            pltpu.VMEM((nh, rl, total), F32),
            pltpu.VMEM((n, rl, total), F32),
            pltpu.VMEM((nc, nh, out_rows, cw), BF),
            pltpu.VMEM((nc, nh, out_rows, cw), BF),
            dma((7,)),
            dma((n,)), dma((n,)),
            dma((nh,)), dma((nh,)),
            dma((n,)), dma((n,)),
            dma((n,)), dma((n,)),
            dma((kvl, n)), dma((kvl, n)),
            dma((nh,)), dma((nh,)),
            dma((n,)), dma((n,)),
            dma((nc, nh)), dma((nc, nh)),
        ],
        compiler_params=pltpu.CompilerParams(
            collective_id=0, has_side_effects=True, vmem_limit_bytes=58 * 1024 * 1024),
    )(
        normed_hidden_rows, base_query, base_key_value,
        cached_length_per_request.reshape(1, rows), request_page_table,
        planned_request_rows.reshape(1, total), request_adapters.reshape(1, total),
        key_value_cache, query_key_value_down_maps, qups, key_value_up_maps,
        output_down_maps, ups, output_weight_matrix,
    )


def solution(mesh):
    return jax.shard_map(
        body,
        mesh=mesh,
        in_specs=(
            P(("groups", "adapter"), "head"),
            P(("groups", "adapter"), "head"),
            P(("groups", "adapter"), None, "head"),
            P(("groups", "adapter"), None, None, "head"),
            P(("groups", "adapter")),
            P(("groups", "adapter"), None),
            P("groups"),
            P("groups"),
            P("adapter", "head", None),
            P("adapter", None, "head"),
            P("adapter", None, None, "head"),
            P("adapter", "head", None),
            P("adapter", "head", None),
            P("head", "adapter"),
        ),
        out_specs=P(("groups", "head"), "adapter"),
        check_vma=False,
    )
```

```python
import functools
import math

import jax
import jax.numpy as jnp
from jax import lax
from jax.experimental import pallas as pl
from jax.experimental.pallas import tpu as pltpu
from jax.sharding import PartitionSpec as P

QH = 64
KVH = 8
HD = 128
BF = jnp.bfloat16
F32 = jnp.float32
I32 = jnp.int32
CHUNK_PAGES = 64


def iota(shape, dim):
    return lax.broadcasted_iota(I32, shape, dim)


def mm(a, b, dims=((1,), (0,))):
    return lax.dot_general(a, b, (dims, ((), ())), preferred_element_type=F32)


def kernel(
    cfg,
    hid_ref, bq_ref, bkv_ref, len_ref, table_ref, plan_ref, reqad_ref,
    cache_hbm, down_hbm, qup_hbm, kvup_hbm, odown_hbm, oup_hbm, w_hbm,
    out_ref,
    cache_v, down_v, qup_v, kvup_v, odown_v, w_v,
    row_out, row_in, ps_out, ps_in, dl_out, dl_in, up_all,
    bias_s, score_s, att, tot, rr_out, rr_in, fin_out, fin_in,
    lsem, row_ss, row_rs, ps_ss, ps_rs, dl_ss, dl_rs, up_ss, up_rs,
    y_ss, y_rs, att_ss, att_rs, rr_ss, rr_rs, fin_ss, fin_rs,
):
    n, nh, rows, slot, na, rank = cfg
    total = n * rows
    cells = n * slot
    group = QH // KVH
    kvl = bkv_ref.shape[2] // HD
    half = group * HD
    qw = kvl * half
    z = lax.axis_index("adapter")
    h = lax.axis_index("head")
    gi = lax.axis_index("groups")
    ng = lax.axis_size("groups")
    me = z * nh + h
    plane = n * nh

    def peer_z(d):
        return lax.rem(z + d, n)

    def peer_h(d):
        return lax.rem(h + d, nh)

    def rcopy(src, dst, ss, rs, axis, dev):
        return pltpu.make_async_remote_copy(
            src_ref=src, dst_ref=dst, send_sem=ss, recv_sem=rs,
            device_id=dev if axis is None else {axis: dev}, device_id_type=pl.DeviceIdType.MESH,
        )

    locals_ = []
    for i, (src, dst) in enumerate((
        (down_hbm, down_v), (qup_hbm, qup_v), (kvup_hbm, kvup_v),
        (cache_hbm, cache_v), (odown_hbm, odown_v), (w_hbm, w_v),
    )):
        cp = pltpu.make_async_copy(src, dst, lsem.at[i])
        cp.start()
        locals_.append(cp)
    own_up = pltpu.make_async_copy(
        oup_hbm.at[:, pl.ds(pl.multiple_of(z * w_v.shape[1], 128), w_v.shape[1])],
        up_all.at[z], lsem.at[6])
    own_up.start()

    barrier = pltpu.get_barrier_semaphore()

    def plane_dev(d):
        other = lax.rem(me + d, plane)
        return other, {"adapter": other // nh, "head": lax.rem(other, nh)}

    @pl.loop(1, plane)
    def _(d):
        pl.semaphore_signal(barrier, inc=1, device_id=plane_dev(d)[1],
                            device_id_type=pl.DeviceIdType.MESH)

    for d in range(1, ng):
        pl.semaphore_signal(barrier, inc=1, device_id={"groups": lax.rem(gi + d, ng)},
                            device_id_type=pl.DeviceIdType.MESH)

    jj = iota((total, total), 0)
    ii = iota((total, total), 1)
    eye = jj == ii

    def to_col(row):
        return jnp.sum(jnp.where(eye, row, 0), axis=1, keepdims=True)

    def to_row(col):
        return jnp.sum(jnp.where(eye, col, 0), axis=0, keepdims=True)

    plan_col = to_col(plan_ref[...])
    ad_col = jnp.sum(jnp.where(plan_col == ii, reqad_ref[...], 0), axis=1, keepdims=True)
    ad_row = to_row(ad_col)
    own_col = ad_col // na
    own_row = ad_row // na
    before = (own_col == own_row) & (jj // rows == ii // rows) & (ii < jj)
    slot_col = jnp.sum(before.astype(I32), axis=1, keepdims=True)
    slot_row = to_row(slot_col)
    target_col = own_col * slot + slot_col
    mine = iota((total, rows), 0) == z * rows + iota((total, rows), 1)
    my_target = jnp.sum(jnp.where(mine, target_col, 0), axis=0, keepdims=True)
    give = (my_target == iota((cells, rows), 0)).astype(F32).astype(BF)
    place_row = (iota((1, total), 1) // rows) * slot + slot_row
    cell_hit = (own_row == z) & (place_row == iota((cells, total), 0))
    local_ad = jnp.sum(jnp.where(cell_hit, ad_row - own_row * na + 1, 0), axis=1, keepdims=True) - 1

    outgoing = mm(give, hid_ref[...]).astype(BF)
    row_out[...] = outgoing.reshape(row_out.shape)
    row_in[z] = row_out[z]

    pl.semaphore_wait(barrier, plane - 1 + ng - 1)

    sends = []
    for d in range(1, n):
        o = peer_z(d)
        cp = rcopy(row_out.at[o], row_in.at[z], row_ss.at[o], row_rs.at[z], "adapter", o)
        cp.start()
        sends.append(cp)

    pages = cache_v.shape[0]
    page_len = cache_v.shape[2]
    ct = CHUNK_PAGES * page_len
    nchunk = pages // CHUNK_PAGES
    table = table_ref[...]
    page_ids = iota((rows, pages), 1)
    pos = jnp.zeros((rows, pages), I32)
    for t in range(table.shape[1]):
        pos = jnp.where(table[:, t:t + 1] == page_ids, t + 1, pos)
    len_col = jnp.sum(jnp.where(iota((rows, rows), 0) == iota((rows, rows), 1), len_ref[...], 0),
                      axis=1, keepdims=True)
    lim = jnp.where(pos > 0, jnp.clip(len_col - page_len * (pos - 1), 0, page_len), 0)
    lim = lim.astype(F32).astype(BF)
    spread = (iota((CHUNK_PAGES, ct), 1) // page_len == iota((CHUNK_PAGES, ct), 0)).astype(F32).astype(BF)
    within_page = lax.rem(iota((rows, ct), 1), page_len).astype(F32)
    for c in range(nchunk):
        wide = mm(lim[:, c * CHUNK_PAGES:(c + 1) * CHUNK_PAGES], spread)
        bias_s[c] = jnp.where(within_page < wide, 0.0, -jnp.inf)

    locals_[0].wait()
    for d in range(1, n):
        o = peer_z(d)
        rcopy(row_out.at[o], row_in.at[o], row_ss.at[o], row_rs.at[o], "adapter", o).wait_recv()

    received = row_in[...].reshape(cells, row_in.shape[2])
    spread_ranks = mm(received, down_v[...], ((1,), (1,)))
    part = jnp.zeros((cells, 3 * rank), F32)
    for a in range(na):
        part = jnp.where(local_ad == a, spread_ranks[:, a * 3 * rank:(a + 1) * 3 * rank], part)
    ps_out[...] = part
    for d in range(1, nh):
        p = peer_h(d)
        cp = rcopy(ps_out, ps_in.at[h], ps_ss.at[p], ps_rs.at[h], "head", p)
        cp.start()
        sends.append(cp)
    cols = w_v.shape[1]
    share = cols // ng

    def up_src(o):
        return oup_hbm.at[:, pl.ds(pl.multiple_of(o * cols + gi * share, 128), share)]

    def up_part(o, who):
        return up_all.at[o, :, pl.ds(pl.multiple_of(who * share, 128), share)]

    for d in range(1, n):
        o = peer_z(d)
        cp = rcopy(up_src(o), up_part(z, gi), up_ss.at[o], up_rs.at[z], "adapter", o)
        cp.start()
        sends.append(cp)
    locals_[1].wait()
    locals_[2].wait()
    for d in range(1, nh):
        p = peer_h(d)
        rcopy(ps_out, ps_in.at[p], ps_ss.at[p], ps_rs.at[p], "head", p).wait_recv()
        part = part + ps_in[p]
    part = part * 0.5

    def chosen(lo):
        piece = part[:, lo:lo + rank]
        return jnp.concatenate(
            [jnp.where(local_ad == a, piece, 0.0) for a in range(na)], axis=1).astype(BF)

    q_sel = chosen(0)
    kv_sel = [chosen((1 + i) * rank) for i in range(2)]
    for k in range(kvl):
        dl_out[k, :, :, :half] = (
            mm(q_sel, qup_v[:, k * half:(k + 1) * half]).astype(BF).reshape(n, slot, half))
        for i in range(2):
            maps = jnp.concatenate(
                [kvup_v[a, i, :, k * HD:(k + 1) * HD] for a in range(na)], axis=0)
            dl_out[k, :, :, half + i * HD:half + (i + 1) * HD] = (
                mm(kv_sel[i], maps).astype(BF).reshape(n, slot, HD))
        dl_in[k, z] = dl_out[k, z]
        for d in range(1, n):
            o = peer_z(d)
            cp = rcopy(dl_out.at[k, o], dl_in.at[k, z], dl_ss.at[k, o], dl_rs.at[k, z], "adapter", o)
            cp.start()
            sends.append(cp)
    eye_r = (iota((rows, total), 0) + z * rows) == iota((rows, total), 1)
    target_row = own_row * slot + slot_row
    take_col = jnp.sum(jnp.where(eye_r, target_row, 0), axis=1, keepdims=True)
    take = (take_col == iota((rows, cells), 1)).astype(F32).astype(BF)
    for d in range(1, n):
        o = peer_z(d)
        rcopy(up_src(o), up_part(o, gi), up_ss.at[o], up_rs.at[o], "adapter", o).wait_recv()
        for e in range(1, ng):
            y = lax.rem(gi + e, ng)
            cp = rcopy(up_part(o, gi), up_part(o, gi), y_ss.at[y, o], y_rs.at[gi, o], "groups", y)
            cp.start()
            sends.append(cp)
    locals_[3].wait()

    scale = HD ** -0.5 * math.log2(math.e)
    gr = group * rows
    for k in range(kvl):
        lanes = slice(k * HD, (k + 1) * HD)
        for d in range(1, n):
            o = peer_z(d)
            rcopy(dl_out.at[k, o], dl_in.at[k, o], dl_ss.at[k, o], dl_rs.at[k, o], "adapter", o).wait_recv()
        delta = mm(take, dl_in[k].reshape(cells, dl_in.shape[3]))
        query = (bq_ref[:, k * half:(k + 1) * half].astype(F32) + delta[:, :half]).astype(BF)
        key_new = (bkv_ref[:, 0, lanes].astype(F32) + delta[:, half:half + HD]).astype(BF).astype(F32)
        value_new = (bkv_ref[:, 1, lanes].astype(F32) + delta[:, half + HD:]).astype(BF).astype(F32)
        qh = jnp.concatenate([query[:, g * HD:(g + 1) * HD] for g in range(group)], axis=0)
        kn = jnp.concatenate([key_new] * group, axis=0)
        vn = jnp.concatenate([value_new] * group, axis=0)
        own = jnp.sum(qh.astype(F32) * kn, axis=1, keepdims=True) * scale

        def scores(c, top):
            keys = cache_v[pl.ds(c * CHUNK_PAGES, CHUNK_PAGES), 0, :, lanes].reshape(ct, HD)
            s = mm(qh, keys, ((1,), (1,))) * scale
            s = (s.reshape(group, rows, ct) + bias_s[c][None]).reshape(gr, ct)
            score_s[c] = s
            for i in range(ct // HD):
                top = jnp.maximum(top, s[:, i * HD:(i + 1) * HD])
            return top

        top = lax.fori_loop(0, nchunk, scores, jnp.full((gr, HD), -jnp.inf, F32))
        top = jnp.maximum(jnp.max(top, axis=1, keepdims=True), own)

        def mix(c, carry):
            acc, den = carry
            w = jnp.exp2(score_s[c] - top)
            for i in range(ct // HD):
                den = den + w[:, i * HD:(i + 1) * HD]
            values = cache_v[pl.ds(c * CHUNK_PAGES, CHUNK_PAGES), 1, :, lanes].reshape(ct, HD)
            return acc + mm(w.astype(BF), values), den

        zero = jnp.zeros((gr, HD), F32)
        acc, den = lax.fori_loop(0, nchunk, mix, (zero, zero))
        own_w = jnp.exp2(own - top)
        den = jnp.sum(den, axis=1, keepdims=True) + own_w
        mixed = ((acc + own_w * vn) / den).astype(BF)
        for g in range(group):
            att[k, z, :, g * HD:(g + 1) * HD] = mixed[g * rows:(g + 1) * rows]
        for d in range(1, n):
            o = peer_z(d)
            cp = rcopy(att.at[k, z], att.at[k, z], att_ss.at[k, o], att_rs.at[k, z], "adapter", o)
            cp.start()
            sends.append(cp)

    locals_[4].wait()
    locals_[5].wait()
    nc, _, cw = tot.shape
    turned = jnp.zeros((na * rank, total), F32)
    for k in range(kvl):
        for d in range(1, n):
            o = peer_z(d)
            rcopy(att.at[k, o], att.at[k, o], att_ss.at[k, o], att_rs.at[k, o], "adapter", o).wait_recv()
        every = att[k].reshape(total, half)
        turned = turned + mm(odown_v[:, k * half:(k + 1) * half], every, ((1,), (1,)))
        if k == kvl - 1:
            turned = jnp.where(ad_row == z * na + iota((na * rank, total), 0) // rank, turned, 0.0)
            ranks = turned[:rank]
            for a in range(1, na):
                ranks = ranks + turned[a * rank:(a + 1) * rank]
            rl = rank // nh
            for p in range(nh):
                rr_out[p] = ranks[p * rl:(p + 1) * rl]
            rr_in[me] = rr_out[h]

            @pl.loop(1, plane)
            def _(d):
                other, dev = plane_dev(d)
                rcopy(rr_out.at[lax.rem(other, nh)], rr_in.at[me],
                      rr_ss.at[other], rr_rs.at[me], None, dev).start()

        for c in range(nc):
            term = mm(every, w_v[k * half:(k + 1) * half, c * cw:(c + 1) * cw])
            if k == 0:
                tot[c] = term
            else:
                tot[c] = tot[c] + term

    for d in range(1, n):
        o = peer_z(d)
        for e in range(1, ng):
            y = lax.rem(gi + e, ng)
            rcopy(up_part(o, y), up_part(o, y), y_ss.at[y, o], y_rs.at[y, o], "groups", y).wait_recv()

    @pl.loop(1, plane)
    def _(d):
        other, dev = plane_dev(d)
        rcopy(rr_out.at[lax.rem(other, nh)], rr_in.at[other],
              rr_ss.at[other], rr_rs.at[other], None, dev).wait()

    own_up.wait()
    mine_ranks = jnp.sum(rr_in[...], axis=0)
    rl = rank // nh
    kk = n * na * rl
    tile = (lax.rem(iota((rl, kk), 1), rl) == iota((rl, kk), 0)).astype(F32).astype(BF)
    sel = mm(mine_ranks.astype(BF), tile, ((0,), (0,)))
    sel = jnp.where(ad_col == iota((total, kk), 1) // rl, sel * 0.5, 0.0).astype(BF)
    out_rows = total // nh
    for c in range(nc):
        ups = up_all[:, :, c * cw:(c + 1) * cw].reshape(kk, cw)
        full = tot[c] + mm(sel, ups)
        tot[c] = full
        fin_out[c] = full.astype(BF).reshape(nh, out_rows, cw)
        for d in range(1, nh):
            p = peer_h(d)
            cp = rcopy(fin_out.at[c, p], fin_in.at[c, h], fin_ss.at[c, p], fin_rs.at[c, h], "head", p)
            cp.start()
            sends.append(cp)
    for c in range(nc):
        res = tot[c, pl.ds(pl.multiple_of(h * out_rows, 8), out_rows), :]
        for d in range(1, nh):
            p = peer_h(d)
            rcopy(fin_out.at[c, p], fin_in.at[c, p], fin_ss.at[c, p], fin_rs.at[c, p], "head", p).wait_recv()
            res = res + fin_in[c, p].astype(F32)
        out_ref[:, c * cw:(c + 1) * cw] = res.astype(BF)
    for cp in sends:
        cp.wait_send()


def body(
    normed_hidden_rows,
    base_query,
    base_key_value,
    key_value_cache,
    cached_length_per_request,
    request_page_table,
    planned_request_rows,
    request_adapters,
    query_key_value_down_maps,
    query_up_maps,
    key_value_up_maps,
    output_down_maps,
    output_up_maps,
    output_weight_matrix,
):
    n = lax.axis_size("adapter")
    nh = lax.axis_size("head")
    ng = lax.axis_size("groups")
    rows, feats = normed_hidden_rows.shape
    total = planned_request_rows.shape[0]
    na, _, rank = output_down_maps.shape
    slot = max(16, 2 * rows // n)
    cells = n * slot
    qw = base_query.shape[1]
    kvw = base_key_value.shape[2]
    kvl = kvw // HD
    half = qw // kvl
    dw = half + 2 * HD
    cols = output_weight_matrix.shape[1]
    cw = min(512, cols)
    nc = cols // cw
    pages, _, page_len, _ = key_value_cache.shape
    ct = CHUNK_PAGES * page_len
    gr = QH // KVH * rows
    out_rows = total // nh
    rl = rank // nh
    vm = pl.BlockSpec(memory_space=pltpu.VMEM)
    hb = pl.BlockSpec(memory_space=pl.ANY)
    dma = pltpu.SemaphoreType.DMA
    ups = output_up_maps.reshape(na * output_up_maps.shape[1], -1)
    downs = jnp.swapaxes(query_key_value_down_maps, 1, 2).reshape(na * 3 * rank, feats)
    odowns = jnp.swapaxes(output_down_maps, 1, 2).reshape(na * rank, qw)
    qups = query_up_maps.reshape(na * rank, qw)
    return pl.pallas_call(
        functools.partial(kernel, (n, nh, rows, slot, na, rank)),
        out_shape=jax.ShapeDtypeStruct((out_rows, cols), BF),
        in_specs=[vm] * 7 + [hb] * 7,
        out_specs=vm,
        scratch_shapes=[
            pltpu.VMEM(key_value_cache.shape, BF),
            pltpu.VMEM(downs.shape, BF),
            pltpu.VMEM(qups.shape, BF),
            pltpu.VMEM(key_value_up_maps.shape, BF),
            pltpu.VMEM(odowns.shape, BF),
            pltpu.VMEM(output_weight_matrix.shape, BF),
            pltpu.VMEM((n, slot, feats), BF),
            pltpu.VMEM((n, slot, feats), BF),
            pltpu.VMEM((cells, 3 * rank), F32),
            pltpu.VMEM((nh, cells, 3 * rank), F32),
            pltpu.VMEM((kvl, n, slot, dw), BF),
            pltpu.VMEM((kvl, n, slot, dw), BF),
            pltpu.VMEM((n, ups.shape[0], cols), BF),
            pltpu.VMEM((pages // CHUNK_PAGES, rows, ct), F32),
            pltpu.VMEM((pages // CHUNK_PAGES, gr, ct), F32),
            pltpu.VMEM((kvl, n, rows, half), BF),
            pltpu.VMEM((nc, total, cw), F32),
            pltpu.VMEM((nh, rl, total), F32),
            pltpu.VMEM((n * nh, rl, total), F32),
            pltpu.VMEM((nc, nh, out_rows, cw), BF),
            pltpu.VMEM((nc, nh, out_rows, cw), BF),
            dma((7,)),
            dma((n,)), dma((n,)),
            dma((nh,)), dma((nh,)),
            dma((kvl, n)), dma((kvl, n)),
            dma((n,)), dma((n,)),
            dma((ng, n)), dma((ng, n)),
            dma((kvl, n)), dma((kvl, n)),
            dma((n * nh,)), dma((n * nh,)),
            dma((nc, nh)), dma((nc, nh)),
        ],
        compiler_params=pltpu.CompilerParams(
            collective_id=0, has_side_effects=True, vmem_limit_bytes=58 * 1024 * 1024),
    )(
        normed_hidden_rows, base_query, base_key_value,
        cached_length_per_request.reshape(1, rows), request_page_table,
        planned_request_rows.reshape(1, total), request_adapters.reshape(1, total),
        key_value_cache, downs, qups, key_value_up_maps,
        odowns, ups, output_weight_matrix,
    )


def solution(mesh):
    return jax.shard_map(
        body,
        mesh=mesh,
        in_specs=(
            P(("groups", "adapter"), "head"),
            P(("groups", "adapter"), "head"),
            P(("groups", "adapter"), None, "head"),
            P(("groups", "adapter"), None, None, "head"),
            P(("groups", "adapter")),
            P(("groups", "adapter"), None),
            P("groups"),
            P("groups"),
            P("adapter", "head", None),
            P("adapter", None, "head"),
            P("adapter", None, None, "head"),
            P("adapter", "head", None),
            P("adapter", "head", None),
            P("head", "adapter"),
        ),
        out_specs=P(("groups", "head"), "adapter"),
        check_vma=False,
    )
```

```python
import functools
import math

import jax
import jax.numpy as jnp
from jax import lax
from jax.experimental import pallas as pl
from jax.experimental.pallas import tpu as pltpu
from jax.sharding import PartitionSpec as P

QH = 64
KVH = 8
HD = 128
BF = jnp.bfloat16
F32 = jnp.float32
I32 = jnp.int32
CHUNK_PAGES = 64


def iota(shape, dim):
    return lax.broadcasted_iota(I32, shape, dim)


def mm(a, b, dims=((1,), (0,))):
    return lax.dot_general(a, b, (dims, ((), ())), preferred_element_type=F32)


def kernel(
    cfg,
    hid_ref, bq_ref, bkv_ref, len_ref, table_ref, plan_ref, reqad_ref,
    cache_hbm, down_hbm, qup_hbm, kvup_hbm, odown_hbm, oup_hbm, w_hbm,
    out_ref,
    cache_v, down_v, qup_v, kvup_v, odown_v, w_v,
    row_out, row_in, ps_out, ps_in, dl_out, dl_in, up_all,
    bias_s, score_s, att, tot, rr_out, rr_in, sa_out, sa_in, fin_out, fin_in,
    lsem, row_ss, row_rs, ps_ss, ps_rs, dl_ss, dl_rs, up_ss, up_rs,
    y_ss, y_rs, att_ss, att_rs, rr_ss, rr_rs, sa_ss, sa_rs, fin_ss, fin_rs,
):
    n, nh, rows, slot, na, rank = cfg
    total = n * rows
    cells = n * slot
    group = QH // KVH
    kvl = bkv_ref.shape[2] // HD
    half = group * HD
    qw = kvl * half
    z = lax.axis_index("adapter")
    h = lax.axis_index("head")
    gi = lax.axis_index("groups")
    ng = lax.axis_size("groups")
    me = z * nh + h
    plane = n * nh

    def peer_z(d):
        return lax.rem(z + d, n)

    def peer_h(d):
        return lax.rem(h + d, nh)

    def rcopy(src, dst, ss, rs, axis, dev):
        return pltpu.make_async_remote_copy(
            src_ref=src, dst_ref=dst, send_sem=ss, recv_sem=rs,
            device_id=dev if axis is None else {axis: dev}, device_id_type=pl.DeviceIdType.MESH,
        )

    locals_ = []
    for i, (src, dst) in enumerate((
        (down_hbm, down_v), (qup_hbm, qup_v), (kvup_hbm, kvup_v),
        (cache_hbm, cache_v), (odown_hbm, odown_v), (w_hbm, w_v),
    )):
        cp = pltpu.make_async_copy(src, dst, lsem.at[i])
        cp.start()
        locals_.append(cp)
    own_up = pltpu.make_async_copy(
        oup_hbm.at[:, pl.ds(pl.multiple_of(z * w_v.shape[1], 128), w_v.shape[1])],
        up_all.at[z], lsem.at[6])
    own_up.start()

    barrier = pltpu.get_barrier_semaphore()

    def plane_dev(d):
        other = lax.rem(me + d, plane)
        return other, {"adapter": other // nh, "head": lax.rem(other, nh)}

    @pl.loop(1, plane)
    def _(d):
        pl.semaphore_signal(barrier, inc=1, device_id=plane_dev(d)[1],
                            device_id_type=pl.DeviceIdType.MESH)

    for d in range(1, ng):
        pl.semaphore_signal(barrier, inc=1, device_id={"groups": lax.rem(gi + d, ng)},
                            device_id_type=pl.DeviceIdType.MESH)

    jj = iota((total, total), 0)
    ii = iota((total, total), 1)
    eye = jj == ii

    def to_col(row):
        return jnp.sum(jnp.where(eye, row, 0), axis=1, keepdims=True)

    def to_row(col):
        return jnp.sum(jnp.where(eye, col, 0), axis=0, keepdims=True)

    plan_col = to_col(plan_ref[...])
    ad_col = jnp.sum(jnp.where(plan_col == ii, reqad_ref[...], 0), axis=1, keepdims=True)
    ad_row = to_row(ad_col)
    own_col = ad_col // na
    own_row = ad_row // na
    before = (own_col == own_row) & (jj // rows == ii // rows) & (ii < jj)
    slot_col = jnp.sum(before.astype(I32), axis=1, keepdims=True)
    slot_row = to_row(slot_col)
    target_col = own_col * slot + slot_col
    mine = iota((total, rows), 0) == z * rows + iota((total, rows), 1)
    my_target = jnp.sum(jnp.where(mine, target_col, 0), axis=0, keepdims=True)
    give = (my_target == iota((cells, rows), 0)).astype(F32).astype(BF)
    place_row = (iota((1, total), 1) // rows) * slot + slot_row
    cell_hit = (own_row == z) & (place_row == iota((cells, total), 0))
    local_ad = jnp.sum(jnp.where(cell_hit, ad_row - own_row * na + 1, 0), axis=1, keepdims=True) - 1

    outgoing = mm(give, hid_ref[...]).astype(BF)
    row_out[...] = outgoing.reshape(row_out.shape)
    row_in[z] = row_out[z]

    pl.semaphore_wait(barrier, plane - 1 + ng - 1)

    sends = []
    for d in range(1, n):
        o = peer_z(d)
        cp = rcopy(row_out.at[o], row_in.at[z], row_ss.at[o], row_rs.at[z], "adapter", o)
        cp.start()
        sends.append(cp)

    pages = cache_v.shape[0]
    page_len = cache_v.shape[2]
    ct = CHUNK_PAGES * page_len
    nchunk = pages // CHUNK_PAGES
    table = table_ref[...]
    page_ids = iota((rows, pages), 1)
    pos = jnp.zeros((rows, pages), I32)
    for t in range(table.shape[1]):
        pos = jnp.where(table[:, t:t + 1] == page_ids, t + 1, pos)
    len_col = jnp.sum(jnp.where(iota((rows, rows), 0) == iota((rows, rows), 1), len_ref[...], 0),
                      axis=1, keepdims=True)
    lim = jnp.where(pos > 0, jnp.clip(len_col - page_len * (pos - 1), 0, page_len), 0)
    lim = lim.astype(F32).astype(BF)
    spread = (iota((CHUNK_PAGES, ct), 1) // page_len == iota((CHUNK_PAGES, ct), 0)).astype(F32).astype(BF)
    within_page = lax.rem(iota((rows, ct), 1), page_len).astype(F32)
    for c in range(nchunk):
        wide = mm(lim[:, c * CHUNK_PAGES:(c + 1) * CHUNK_PAGES], spread)
        bias_s[c] = jnp.where(within_page < wide, 0.0, -jnp.inf)

    locals_[0].wait()
    for d in range(1, n):
        o = peer_z(d)
        rcopy(row_out.at[o], row_in.at[o], row_ss.at[o], row_rs.at[o], "adapter", o).wait_recv()

    received = row_in[...].reshape(cells, row_in.shape[2])
    spread_ranks = mm(received, down_v[...], ((1,), (1,)))
    part = jnp.zeros((cells, 3 * rank), F32)
    for a in range(na):
        part = jnp.where(local_ad == a, spread_ranks[:, a * 3 * rank:(a + 1) * 3 * rank], part)
    ps_out[...] = part
    for d in range(1, nh):
        p = peer_h(d)
        cp = rcopy(ps_out, ps_in.at[h], ps_ss.at[p], ps_rs.at[h], "head", p)
        cp.start()
        sends.append(cp)
    cols = w_v.shape[1]
    share = cols // ng

    def up_src(o):
        return oup_hbm.at[:, pl.ds(pl.multiple_of(o * cols + gi * share, 128), share)]

    def up_part(o, who):
        return up_all.at[o, :, pl.ds(pl.multiple_of(who * share, 128), share)]

    for d in range(1, n):
        o = peer_z(d)
        cp = rcopy(up_src(o), up_part(z, gi), up_ss.at[o], up_rs.at[z], "adapter", o)
        cp.start()
        sends.append(cp)
    locals_[1].wait()
    locals_[2].wait()
    for d in range(1, nh):
        p = peer_h(d)
        rcopy(ps_out, ps_in.at[p], ps_ss.at[p], ps_rs.at[p], "head", p).wait_recv()
        part = part + ps_in[p]
    part = part * 0.5

    def chosen(lo):
        piece = part[:, lo:lo + rank]
        return jnp.concatenate(
            [jnp.where(local_ad == a, piece, 0.0) for a in range(na)], axis=1).astype(BF)

    q_sel = chosen(0)
    kv_sel = [chosen((1 + i) * rank) for i in range(2)]
    for k in range(kvl):
        dl_out[k, :, :, :half] = (
            mm(q_sel, qup_v[:, k * half:(k + 1) * half]).astype(BF).reshape(n, slot, half))
        for i in range(2):
            maps = jnp.concatenate(
                [kvup_v[a, i, :, k * HD:(k + 1) * HD] for a in range(na)], axis=0)
            dl_out[k, :, :, half + i * HD:half + (i + 1) * HD] = (
                mm(kv_sel[i], maps).astype(BF).reshape(n, slot, HD))
        dl_in[k, z] = dl_out[k, z]
        for d in range(1, n):
            o = peer_z(d)
            cp = rcopy(dl_out.at[k, o], dl_in.at[k, z], dl_ss.at[k, o], dl_rs.at[k, z], "adapter", o)
            cp.start()
            sends.append(cp)
    eye_r = (iota((rows, total), 0) + z * rows) == iota((rows, total), 1)
    target_row = own_row * slot + slot_row
    take_col = jnp.sum(jnp.where(eye_r, target_row, 0), axis=1, keepdims=True)
    take = (take_col == iota((rows, cells), 1)).astype(F32).astype(BF)
    for d in range(1, n):
        o = peer_z(d)
        rcopy(up_src(o), up_part(o, gi), up_ss.at[o], up_rs.at[o], "adapter", o).wait_recv()
        for e in range(1, ng):
            y = lax.rem(gi + e, ng)
            cp = rcopy(up_part(o, gi), up_part(o, gi), y_ss.at[y, o], y_rs.at[gi, o], "groups", y)
            cp.start()
            sends.append(cp)
    locals_[3].wait()

    def hop(k, o, way):
        to = lax.rem(z + 1, n) if way == 0 else lax.rem(z + n - 1, n)
        return rcopy(att.at[k, o], att.at[k, o], att_ss.at[way, k, o], att_rs.at[k, o], "adapter", to)

    def arrive(k, d):
        low = jnp.maximum(z - d, 0)
        high = jnp.minimum(z + d, n - 1)

        @pl.when(z >= d)
        def _():
            hop(k, low, 0).wait_recv()

        @pl.when((z >= d) & (z < n - 1))
        def _():
            hop(k, low, 0).start()

        @pl.when(z + d < n)
        def _():
            hop(k, high, 1).wait_recv()

        @pl.when((z + d < n) & (z > 0))
        def _():
            hop(k, high, 1).start()

    scale = HD ** -0.5 * math.log2(math.e)
    gr = group * rows
    for k in range(kvl):
        lanes = slice(k * HD, (k + 1) * HD)
        for d in range(1, n):
            o = peer_z(d)
            rcopy(dl_out.at[k, o], dl_in.at[k, o], dl_ss.at[k, o], dl_rs.at[k, o], "adapter", o).wait_recv()
        delta = mm(take, dl_in[k].reshape(cells, dl_in.shape[3]))
        query = (bq_ref[:, k * half:(k + 1) * half].astype(F32) + delta[:, :half]).astype(BF)
        key_new = (bkv_ref[:, 0, lanes].astype(F32) + delta[:, half:half + HD]).astype(BF).astype(F32)
        value_new = (bkv_ref[:, 1, lanes].astype(F32) + delta[:, half + HD:]).astype(BF).astype(F32)
        qh = jnp.concatenate([query[:, g * HD:(g + 1) * HD] for g in range(group)], axis=0)
        kn = jnp.concatenate([key_new] * group, axis=0)
        vn = jnp.concatenate([value_new] * group, axis=0)
        own = jnp.sum(qh.astype(F32) * kn, axis=1, keepdims=True) * scale

        def scores(c, top):
            keys = cache_v[pl.ds(c * CHUNK_PAGES, CHUNK_PAGES), 0, :, lanes].reshape(ct, HD)
            s = mm(qh, keys, ((1,), (1,))) * scale
            s = (s.reshape(group, rows, ct) + bias_s[c][None]).reshape(gr, ct)
            score_s[c] = s
            for i in range(ct // HD):
                top = jnp.maximum(top, s[:, i * HD:(i + 1) * HD])
            return top

        top = lax.fori_loop(0, nchunk, scores, jnp.full((gr, HD), -jnp.inf, F32))
        top = jnp.maximum(jnp.max(top, axis=1, keepdims=True), own)

        def mix(c, carry):
            acc, den = carry
            w = jnp.exp2(score_s[c] - top)
            for i in range(ct // HD):
                den = den + w[:, i * HD:(i + 1) * HD]
            values = cache_v[pl.ds(c * CHUNK_PAGES, CHUNK_PAGES), 1, :, lanes].reshape(ct, HD)
            return acc + mm(w.astype(BF), values), den

        zero = jnp.zeros((gr, HD), F32)
        acc, den = lax.fori_loop(0, nchunk, mix, (zero, zero))
        own_w = jnp.exp2(own - top)
        den = jnp.sum(den, axis=1, keepdims=True) + own_w
        mixed = ((acc + own_w * vn) / den).astype(BF)
        for g in range(group):
            att[k, z, :, g * HD:(g + 1) * HD] = mixed[g * rows:(g + 1) * rows]
        pl.when(z < n - 1)(lambda k=k: hop(k, z, 0).start())
        pl.when(z > 0)(lambda k=k: hop(k, z, 1).start())

    locals_[4].wait()
    locals_[5].wait()
    nc, _, cw = tot.shape
    turned = jnp.zeros((na * rank, total), F32)
    for d in range(1, n):
        for k in range(kvl if d < n - 1 else 1):
            arrive(k, d)
    for k in range(kvl):
        if k > 0:
            arrive(k, n - 1)
        every = att[k].reshape(total, half)
        turned = turned + mm(odown_v[:, k * half:(k + 1) * half], every, ((1,), (1,)))
        if k == kvl - 1:
            turned = jnp.where(ad_row == z * na + iota((na * rank, total), 0) // rank, turned, 0.0)
            ranks = turned[:rank]
            for a in range(1, na):
                ranks = ranks + turned[a * rank:(a + 1) * rank]
            rl = rank // nh
            for p in range(nh):
                rr_out[p] = ranks[p * rl:(p + 1) * rl]
            rr_in[me] = rr_out[h]

            @pl.loop(1, plane)
            def _(d):
                other, dev = plane_dev(d)
                rcopy(rr_out.at[lax.rem(other, nh)], rr_in.at[me],
                      rr_ss.at[other], rr_rs.at[me], None, dev).start()

        for c in range(nc):
            term = mm(every, w_v[k * half:(k + 1) * half, c * cw:(c + 1) * cw])
            if k == 0:
                tot[c] = term
            else:
                tot[c] = tot[c] + term

    for d in range(1, n):
        o = peer_z(d)
        for e in range(1, ng):
            y = lax.rem(gi + e, ng)
            rcopy(up_part(o, y), up_part(o, y), y_ss.at[y, o], y_rs.at[y, o], "groups", y).wait_recv()

    @pl.loop(1, plane)
    def _(d):
        other, dev = plane_dev(d)
        rcopy(rr_out.at[lax.rem(other, nh)], rr_in.at[other],
              rr_ss.at[other], rr_rs.at[other], None, dev).wait()

    own_up.wait()
    mine_ranks = jnp.sum(rr_in[...], axis=0)
    rl = rank // nh
    kk = n * na * rl
    tile = (lax.rem(iota((rl, kk), 1), rl) == iota((rl, kk), 0)).astype(F32).astype(BF)
    sel = mm(mine_ranks.astype(BF), tile, ((0,), (0,)))
    sel = jnp.where(ad_col == iota((total, kk), 1) // rl, sel * 0.5, 0.0).astype(BF)
    out_rows = total // nh
    nx = nh // 2
    xi = h // 2
    core = lax.rem(h, 2)
    sibling = 2 * xi + 1 - core

    def block(c, p):
        return tot[c, pl.ds(pl.multiple_of(p * out_rows, 8), out_rows), :]

    for c in range(nc):
        ups = up_all[:, :, c * cw:(c + 1) * cw].reshape(kk, cw)
        full = tot[c] + mm(sel, ups)
        tot[c] = full
        for x in range(nx):
            sa_out[c, x] = block(c, 2 * x + 1 - core).astype(BF)
        cp = rcopy(sa_out.at[c], sa_in.at[c], sa_ss.at[c], sa_rs.at[c], "head", sibling)
        cp.start()
        sends.append(cp)
    for c in range(nc):
        rcopy(sa_out.at[c], sa_in.at[c], sa_ss.at[c], sa_rs.at[c], "head", sibling).wait_recv()
        for d in range(1, nx):
            x = lax.rem(xi + d, nx)
            fin_out[c, x] = (block(c, 2 * x + core) + sa_in[c, x].astype(F32)).astype(BF)
            cp = rcopy(fin_out.at[c, x], fin_in.at[c, xi], fin_ss.at[c, x], fin_rs.at[c, xi],
                       "head", 2 * x + core)
            cp.start()
            sends.append(cp)
    for c in range(nc):
        res = block(c, h) + sa_in[c, xi].astype(F32)
        for d in range(1, nx):
            x = lax.rem(xi + d, nx)
            rcopy(fin_out.at[c, x], fin_in.at[c, x], fin_ss.at[c, x], fin_rs.at[c, x],
                  "head", 2 * x + core).wait_recv()
            res = res + fin_in[c, x].astype(F32)
        out_ref[:, c * cw:(c + 1) * cw] = res.astype(BF)
    for k in range(kvl):
        pl.when(z < n - 1)(lambda k=k: hop(k, z, 0).wait_send())
        pl.when(z > 0)(lambda k=k: hop(k, z, 1).wait_send())
        for d in range(1, n):
            pl.when((z >= d) & (z < n - 1))(
                lambda k=k, d=d: hop(k, jnp.maximum(z - d, 0), 0).wait_send())
            pl.when((z + d < n) & (z > 0))(
                lambda k=k, d=d: hop(k, jnp.minimum(z + d, n - 1), 1).wait_send())
    for cp in sends:
        cp.wait_send()


def body(
    normed_hidden_rows,
    base_query,
    base_key_value,
    key_value_cache,
    cached_length_per_request,
    request_page_table,
    planned_request_rows,
    request_adapters,
    query_key_value_down_maps,
    query_up_maps,
    key_value_up_maps,
    output_down_maps,
    output_up_maps,
    output_weight_matrix,
):
    n = lax.axis_size("adapter")
    nh = lax.axis_size("head")
    ng = lax.axis_size("groups")
    rows, feats = normed_hidden_rows.shape
    total = planned_request_rows.shape[0]
    na, _, rank = output_down_maps.shape
    slot = max(16, 2 * rows // n)
    cells = n * slot
    qw = base_query.shape[1]
    kvw = base_key_value.shape[2]
    kvl = kvw // HD
    half = qw // kvl
    dw = half + 2 * HD
    cols = output_weight_matrix.shape[1]
    cw = min(512, cols)
    nc = cols // cw
    pages, _, page_len, _ = key_value_cache.shape
    ct = CHUNK_PAGES * page_len
    gr = QH // KVH * rows
    out_rows = total // nh
    rl = rank // nh
    vm = pl.BlockSpec(memory_space=pltpu.VMEM)
    hb = pl.BlockSpec(memory_space=pl.ANY)
    dma = pltpu.SemaphoreType.DMA
    ups = output_up_maps.reshape(na * output_up_maps.shape[1], -1)
    downs = jnp.swapaxes(query_key_value_down_maps, 1, 2).reshape(na * 3 * rank, feats)
    odowns = jnp.swapaxes(output_down_maps, 1, 2).reshape(na * rank, qw)
    qups = query_up_maps.reshape(na * rank, qw)
    return pl.pallas_call(
        functools.partial(kernel, (n, nh, rows, slot, na, rank)),
        out_shape=jax.ShapeDtypeStruct((out_rows, cols), BF),
        in_specs=[vm] * 7 + [hb] * 7,
        out_specs=vm,
        scratch_shapes=[
            pltpu.VMEM(key_value_cache.shape, BF),
            pltpu.VMEM(downs.shape, BF),
            pltpu.VMEM(qups.shape, BF),
            pltpu.VMEM(key_value_up_maps.shape, BF),
            pltpu.VMEM(odowns.shape, BF),
            pltpu.VMEM(output_weight_matrix.shape, BF),
            pltpu.VMEM((n, slot, feats), BF),
            pltpu.VMEM((n, slot, feats), BF),
            pltpu.VMEM((cells, 3 * rank), F32),
            pltpu.VMEM((nh, cells, 3 * rank), F32),
            pltpu.VMEM((kvl, n, slot, dw), BF),
            pltpu.VMEM((kvl, n, slot, dw), BF),
            pltpu.VMEM((n, ups.shape[0], cols), BF),
            pltpu.VMEM((pages // CHUNK_PAGES, rows, ct), F32),
            pltpu.VMEM((pages // CHUNK_PAGES, gr, ct), F32),
            pltpu.VMEM((kvl, n, rows, half), BF),
            pltpu.VMEM((nc, total, cw), F32),
            pltpu.VMEM((nh, rl, total), F32),
            pltpu.VMEM((n * nh, rl, total), F32),
            pltpu.VMEM((nc, nh // 2, out_rows, cw), BF),
            pltpu.VMEM((nc, nh // 2, out_rows, cw), BF),
            pltpu.VMEM((nc, nh // 2, out_rows, cw), BF),
            pltpu.VMEM((nc, nh // 2, out_rows, cw), BF),
            dma((7,)),
            dma((n,)), dma((n,)),
            dma((nh,)), dma((nh,)),
            dma((kvl, n)), dma((kvl, n)),
            dma((n,)), dma((n,)),
            dma((ng, n)), dma((ng, n)),
            dma((2, kvl, n)), dma((kvl, n)),
            dma((n * nh,)), dma((n * nh,)),
            dma((nc,)), dma((nc,)),
            dma((nc, nh // 2)), dma((nc, nh // 2)),
        ],
        compiler_params=pltpu.CompilerParams(
            collective_id=0, has_side_effects=True, vmem_limit_bytes=58 * 1024 * 1024),
    )(
        normed_hidden_rows, base_query, base_key_value,
        cached_length_per_request.reshape(1, rows), request_page_table,
        planned_request_rows.reshape(1, total), request_adapters.reshape(1, total),
        key_value_cache, downs, qups, key_value_up_maps,
        odowns, ups, output_weight_matrix,
    )


def solution(mesh):
    return jax.shard_map(
        body,
        mesh=mesh,
        in_specs=(
            P(("groups", "adapter"), "head"),
            P(("groups", "adapter"), "head"),
            P(("groups", "adapter"), None, "head"),
            P(("groups", "adapter"), None, None, "head"),
            P(("groups", "adapter")),
            P(("groups", "adapter"), None),
            P("groups"),
            P("groups"),
            P("adapter", "head", None),
            P("adapter", None, "head"),
            P("adapter", None, None, "head"),
            P("adapter", "head", None),
            P("adapter", "head", None),
            P("head", "adapter"),
        ),
        out_specs=P(("groups", "head"), "adapter"),
        check_vma=False,
    )
```

```python
import functools
import math

import jax
import jax.numpy as jnp
from jax import lax
from jax.experimental import pallas as pl
from jax.experimental.pallas import tpu as pltpu
from jax.sharding import PartitionSpec as P

QH = 64
KVH = 8
HD = 128
BF = jnp.bfloat16
F32 = jnp.float32
I32 = jnp.int32
CHUNK_PAGES = 64


def iota(shape, dim):
    return lax.broadcasted_iota(I32, shape, dim)


def mm(a, b, dims=((1,), (0,))):
    return lax.dot_general(a, b, (dims, ((), ())), preferred_element_type=F32)


def kernel(
    cfg,
    hid_ref, bq_ref, bkv_ref, len_ref, table_ref, plan_ref, reqad_ref,
    cache_hbm, down_hbm, qup_hbm, kvup_hbm, odown_hbm, oup_hbm, w_hbm,
    out_ref,
    cache_v, down_v, qup_v, kvup_v, odown_v, w_v,
    row_out, row_in, ps_out, ps_in, dl_out, dl_in, up_all,
    bias_s, score_s, att, tot, rr_out, rr_in, sa_out, sa_in, fin_out, fin_in,
    lsem, row_ss, row_rs, ps_ss, ps_rs, dl_ss, dl_rs, up_ss, up_rs,
    y_ss, y_rs, att_ss, att_rs, rr_ss, rr_rs, sa_ss, sa_rs, fin_ss, fin_rs,
):
    n, nh, rows, slot, na, rank = cfg
    total = n * rows
    cells = n * slot
    group = QH // KVH
    kvl = bkv_ref.shape[2] // HD
    half = group * HD
    qw = kvl * half
    z = lax.axis_index("adapter")
    h = lax.axis_index("head")
    gi = lax.axis_index("groups")
    ng = lax.axis_size("groups")
    me = z * nh + h
    plane = n * nh

    def peer_z(d):
        return lax.rem(z + d, n)

    def peer_h(d):
        return lax.rem(h + d, nh)

    def rcopy(src, dst, ss, rs, axis, dev):
        return pltpu.make_async_remote_copy(
            src_ref=src, dst_ref=dst, send_sem=ss, recv_sem=rs,
            device_id=dev if axis is None else {axis: dev}, device_id_type=pl.DeviceIdType.MESH,
        )

    locals_ = []
    for i, (src, dst) in enumerate((
        (down_hbm, down_v), (qup_hbm, qup_v), (kvup_hbm, kvup_v),
        (cache_hbm, cache_v), (odown_hbm, odown_v), (w_hbm, w_v),
    )):
        cp = pltpu.make_async_copy(src, dst, lsem.at[i])
        if i < 3:
            cp.start()
        locals_.append(cp)
    own_up = pltpu.make_async_copy(
        oup_hbm.at[:, pl.ds(pl.multiple_of(z * w_v.shape[1], 128), w_v.shape[1])],
        up_all.at[z], lsem.at[6])

    barrier = pltpu.get_barrier_semaphore()

    def plane_dev(d):
        other = lax.rem(me + d, plane)
        return other, {"adapter": other // nh, "head": lax.rem(other, nh)}

    @pl.loop(1, plane)
    def _(d):
        pl.semaphore_signal(barrier, inc=1, device_id=plane_dev(d)[1],
                            device_id_type=pl.DeviceIdType.MESH)

    for d in range(1, ng):
        pl.semaphore_signal(barrier, inc=1, device_id={"groups": lax.rem(gi + d, ng)},
                            device_id_type=pl.DeviceIdType.MESH)

    jj = iota((total, total), 0)
    ii = iota((total, total), 1)
    eye = jj == ii

    def to_col(row):
        return jnp.sum(jnp.where(eye, row, 0), axis=1, keepdims=True)

    def to_row(col):
        return jnp.sum(jnp.where(eye, col, 0), axis=0, keepdims=True)

    plan_col = to_col(plan_ref[...])
    ad_col = jnp.sum(jnp.where(plan_col == ii, reqad_ref[...], 0), axis=1, keepdims=True)
    ad_row = to_row(ad_col)
    own_col = ad_col // na
    own_row = ad_row // na
    before = (own_col == own_row) & (jj // rows == ii // rows) & (ii < jj)
    slot_col = jnp.sum(before.astype(I32), axis=1, keepdims=True)
    slot_row = to_row(slot_col)
    target_col = own_col * slot + slot_col
    mine = iota((total, rows), 0) == z * rows + iota((total, rows), 1)
    my_target = jnp.sum(jnp.where(mine, target_col, 0), axis=0, keepdims=True)
    give = (my_target == iota((cells, rows), 0)).astype(F32).astype(BF)
    place_row = (iota((1, total), 1) // rows) * slot + slot_row
    cell_hit = (own_row == z) & (place_row == iota((cells, total), 0))
    local_ad = jnp.sum(jnp.where(cell_hit, ad_row - own_row * na + 1, 0), axis=1, keepdims=True) - 1

    outgoing = mm(give, hid_ref[...]).astype(BF)
    row_out[...] = outgoing.reshape(row_out.shape)
    row_in[z] = row_out[z]

    pl.semaphore_wait(barrier, plane - 1 + ng - 1)

    sends = []
    for d in range(1, n):
        o = peer_z(d)
        cp = rcopy(row_out.at[o], row_in.at[z], row_ss.at[o], row_rs.at[z], "adapter", o)
        cp.start()
        sends.append(cp)

    for cp in locals_[3:]:
        cp.start()
    own_up.start()

    pages = cache_v.shape[0]
    page_len = cache_v.shape[2]
    ct = CHUNK_PAGES * page_len
    nchunk = pages // CHUNK_PAGES
    table = table_ref[...]
    page_ids = iota((rows, pages), 1)
    pos = jnp.zeros((rows, pages), I32)
    for t in range(table.shape[1]):
        pos = jnp.where(table[:, t:t + 1] == page_ids, t + 1, pos)
    len_col = jnp.sum(jnp.where(iota((rows, rows), 0) == iota((rows, rows), 1), len_ref[...], 0),
                      axis=1, keepdims=True)
    lim = jnp.where(pos > 0, jnp.clip(len_col - page_len * (pos - 1), 0, page_len), 0)
    lim = lim.astype(F32).astype(BF)
    spread = (iota((CHUNK_PAGES, ct), 1) // page_len == iota((CHUNK_PAGES, ct), 0)).astype(F32).astype(BF)
    within_page = lax.rem(iota((rows, ct), 1), page_len).astype(F32)
    for c in range(nchunk):
        wide = mm(lim[:, c * CHUNK_PAGES:(c + 1) * CHUNK_PAGES], spread)
        bias_s[c] = jnp.where(within_page < wide, 0.0, -jnp.inf)

    locals_[0].wait()
    for d in range(1, n):
        o = peer_z(d)
        rcopy(row_out.at[o], row_in.at[o], row_ss.at[o], row_rs.at[o], "adapter", o).wait_recv()

    received = row_in[...].reshape(cells, row_in.shape[2])
    spread_ranks = mm(received, down_v[...], ((1,), (1,)))
    part = jnp.zeros((cells, 3 * rank), F32)
    for a in range(na):
        part = jnp.where(local_ad == a, spread_ranks[:, a * 3 * rank:(a + 1) * 3 * rank], part)
    ps_out[...] = part
    for d in range(1, nh):
        p = peer_h(d)
        cp = rcopy(ps_out, ps_in.at[h], ps_ss.at[p], ps_rs.at[h], "head", p)
        cp.start()
        sends.append(cp)
    cols = w_v.shape[1]
    share = cols // ng

    def up_src(o):
        return oup_hbm.at[:, pl.ds(pl.multiple_of(o * cols + gi * share, 128), share)]

    def up_part(o, who):
        return up_all.at[o, :, pl.ds(pl.multiple_of(who * share, 128), share)]

    for d in range(1, n):
        o = peer_z(d)
        cp = rcopy(up_src(o), up_part(z, gi), up_ss.at[o], up_rs.at[z], "adapter", o)
        cp.start()
        sends.append(cp)
    locals_[1].wait()
    locals_[2].wait()
    for d in range(1, nh):
        p = peer_h(d)
        rcopy(ps_out, ps_in.at[p], ps_ss.at[p], ps_rs.at[p], "head", p).wait_recv()
        part = part + ps_in[p]
    part = part * 0.5

    def chosen(lo):
        piece = part[:, lo:lo + rank]
        return jnp.concatenate(
            [jnp.where(local_ad == a, piece, 0.0) for a in range(na)], axis=1).astype(BF)

    q_sel = chosen(0)
    kv_sel = [chosen((1 + i) * rank) for i in range(2)]
    for k in range(kvl):
        dl_out[k, :, :, :half] = (
            mm(q_sel, qup_v[:, k * half:(k + 1) * half]).astype(BF).reshape(n, slot, half))
        for i in range(2):
            maps = jnp.concatenate(
                [kvup_v[a, i, :, k * HD:(k + 1) * HD] for a in range(na)], axis=0)
            dl_out[k, :, :, half + i * HD:half + (i + 1) * HD] = (
                mm(kv_sel[i], maps).astype(BF).reshape(n, slot, HD))
        dl_in[k, z] = dl_out[k, z]
        for d in range(1, n):
            o = peer_z(d)
            cp = rcopy(dl_out.at[k, o], dl_in.at[k, z], dl_ss.at[k, o], dl_rs.at[k, z], "adapter", o)
            cp.start()
            sends.append(cp)
    eye_r = (iota((rows, total), 0) + z * rows) == iota((rows, total), 1)
    target_row = own_row * slot + slot_row
    take_col = jnp.sum(jnp.where(eye_r, target_row, 0), axis=1, keepdims=True)
    take = (take_col == iota((rows, cells), 1)).astype(F32).astype(BF)
    for d in range(1, n):
        o = peer_z(d)
        rcopy(up_src(o), up_part(o, gi), up_ss.at[o], up_rs.at[o], "adapter", o).wait_recv()
        for e in range(1, ng):
            y = lax.rem(gi + e, ng)
            cp = rcopy(up_part(o, gi), up_part(o, gi), y_ss.at[y, o], y_rs.at[gi, o], "groups", y)
            cp.start()
            sends.append(cp)
    locals_[3].wait()

    def hop(k, o, way):
        to = lax.rem(z + 1, n) if way == 0 else lax.rem(z + n - 1, n)
        return rcopy(att.at[k, o], att.at[k, o], att_ss.at[way, k, o], att_rs.at[k, o], "adapter", to)

    def arrive(k, d):
        low = jnp.maximum(z - d, 0)
        high = jnp.minimum(z + d, n - 1)

        @pl.when(z >= d)
        def _():
            hop(k, low, 0).wait_recv()

        @pl.when((z >= d) & (z < n - 1))
        def _():
            hop(k, low, 0).start()

        @pl.when(z + d < n)
        def _():
            hop(k, high, 1).wait_recv()

        @pl.when((z + d < n) & (z > 0))
        def _():
            hop(k, high, 1).start()

    scale = HD ** -0.5 * math.log2(math.e)
    gr = group * rows
    for k in range(kvl):
        lanes = slice(k * HD, (k + 1) * HD)
        for d in range(1, n):
            o = peer_z(d)
            rcopy(dl_out.at[k, o], dl_in.at[k, o], dl_ss.at[k, o], dl_rs.at[k, o], "adapter", o).wait_recv()
        delta = mm(take, dl_in[k].reshape(cells, dl_in.shape[3]))
        query = (bq_ref[:, k * half:(k + 1) * half].astype(F32) + delta[:, :half]).astype(BF)
        key_new = (bkv_ref[:, 0, lanes].astype(F32) + delta[:, half:half + HD]).astype(BF).astype(F32)
        value_new = (bkv_ref[:, 1, lanes].astype(F32) + delta[:, half + HD:]).astype(BF).astype(F32)
        qh = jnp.concatenate([query[:, g * HD:(g + 1) * HD] for g in range(group)], axis=0)
        kn = jnp.concatenate([key_new] * group, axis=0)
        vn = jnp.concatenate([value_new] * group, axis=0)
        own = jnp.sum(qh.astype(F32) * kn, axis=1, keepdims=True) * scale

        def scores(c, top):
            keys = cache_v[pl.ds(c * CHUNK_PAGES, CHUNK_PAGES), 0, :, lanes].reshape(ct, HD)
            s = mm(qh, keys, ((1,), (1,))) * scale
            s = (s.reshape(group, rows, ct) + bias_s[c][None]).reshape(gr, ct)
            score_s[c] = s
            for i in range(ct // HD):
                top = jnp.maximum(top, s[:, i * HD:(i + 1) * HD])
            return top

        top = lax.fori_loop(0, nchunk, scores, jnp.full((gr, HD), -jnp.inf, F32))
        top = jnp.maximum(jnp.max(top, axis=1, keepdims=True), own)

        def mix(c, carry):
            acc, den = carry
            w = jnp.exp2(score_s[c] - top)
            for i in range(ct // HD):
                den = den + w[:, i * HD:(i + 1) * HD]
            values = cache_v[pl.ds(c * CHUNK_PAGES, CHUNK_PAGES), 1, :, lanes].reshape(ct, HD)
            return acc + mm(w.astype(BF), values), den

        zero = jnp.zeros((gr, HD), F32)
        acc, den = lax.fori_loop(0, nchunk, mix, (zero, zero))
        own_w = jnp.exp2(own - top)
        den = jnp.sum(den, axis=1, keepdims=True) + own_w
        mixed = ((acc + own_w * vn) / den).astype(BF)
        for g in range(group):
            att[k, z, :, g * HD:(g + 1) * HD] = mixed[g * rows:(g + 1) * rows]
        pl.when(z < n - 1)(lambda k=k: hop(k, z, 0).start())
        pl.when(z > 0)(lambda k=k: hop(k, z, 1).start())

    locals_[4].wait()
    locals_[5].wait()
    nc, _, cw = tot.shape
    turned = jnp.zeros((na * rank, total), F32)
    for d in range(1, n):
        for k in range(kvl if d < n - 1 else 1):
            arrive(k, d)
    for k in range(kvl):
        if k > 0:
            arrive(k, n - 1)
        every = att[k].reshape(total, half)
        turned = turned + mm(odown_v[:, k * half:(k + 1) * half], every, ((1,), (1,)))
        if k == kvl - 1:
            turned = jnp.where(ad_row == z * na + iota((na * rank, total), 0) // rank, turned, 0.0)
            ranks = turned[:rank]
            for a in range(1, na):
                ranks = ranks + turned[a * rank:(a + 1) * rank]
            rl = rank // nh
            for p in range(nh):
                rr_out[p] = ranks[p * rl:(p + 1) * rl]
            rr_in[me] = rr_out[h]

            @pl.loop(1, plane)
            def _(d):
                other, dev = plane_dev(d)
                rcopy(rr_out.at[lax.rem(other, nh)], rr_in.at[me],
                      rr_ss.at[other], rr_rs.at[me], None, dev).start()

        for c in range(nc):
            term = mm(every, w_v[k * half:(k + 1) * half, c * cw:(c + 1) * cw])
            if k == 0:
                tot[c] = term
            else:
                tot[c] = tot[c] + term

    for d in range(1, n):
        o = peer_z(d)
        for e in range(1, ng):
            y = lax.rem(gi + e, ng)
            rcopy(up_part(o, y), up_part(o, y), y_ss.at[y, o], y_rs.at[y, o], "groups", y).wait_recv()

    @pl.loop(1, plane)
    def _(d):
        other, dev = plane_dev(d)
        rcopy(rr_out.at[lax.rem(other, nh)], rr_in.at[other],
              rr_ss.at[other], rr_rs.at[other], None, dev).wait()

    own_up.wait()
    mine_ranks = jnp.sum(rr_in[...], axis=0)
    rl = rank // nh
    kk = n * na * rl
    tile = (lax.rem(iota((rl, kk), 1), rl) == iota((rl, kk), 0)).astype(F32).astype(BF)
    sel = mm(mine_ranks.astype(BF), tile, ((0,), (0,)))
    sel = jnp.where(ad_col == iota((total, kk), 1) // rl, sel * 0.5, 0.0).astype(BF)
    out_rows = total // nh
    nx = nh // 2
    xi = h // 2
    core = lax.rem(h, 2)
    sibling = 2 * xi + 1 - core

    def block(c, p):
        return tot[c, pl.ds(pl.multiple_of(p * out_rows, 8), out_rows), :]

    for c in range(nc):
        ups = up_all[:, :, c * cw:(c + 1) * cw].reshape(kk, cw)
        full = tot[c] + mm(sel, ups)
        tot[c] = full
        for x in range(nx):
            sa_out[c, x] = block(c, 2 * x + 1 - core).astype(BF)
        cp = rcopy(sa_out.at[c], sa_in.at[c], sa_ss.at[c], sa_rs.at[c], "head", sibling)
        cp.start()
        sends.append(cp)
    for c in range(nc):
        rcopy(sa_out.at[c], sa_in.at[c], sa_ss.at[c], sa_rs.at[c], "head", sibling).wait_recv()
        for d in range(1, nx):
            x = lax.rem(xi + d, nx)
            fin_out[c, x] = (block(c, 2 * x + core) + sa_in[c, x].astype(F32)).astype(BF)
            cp = rcopy(fin_out.at[c, x], fin_in.at[c, xi], fin_ss.at[c, x], fin_rs.at[c, xi],
                       "head", 2 * x + core)
            cp.start()
            sends.append(cp)
    for c in range(nc):
        res = block(c, h) + sa_in[c, xi].astype(F32)
        for d in range(1, nx):
            x = lax.rem(xi + d, nx)
            rcopy(fin_out.at[c, x], fin_in.at[c, x], fin_ss.at[c, x], fin_rs.at[c, x],
                  "head", 2 * x + core).wait_recv()
            res = res + fin_in[c, x].astype(F32)
        out_ref[:, c * cw:(c + 1) * cw] = res.astype(BF)
    for k in range(kvl):
        pl.when(z < n - 1)(lambda k=k: hop(k, z, 0).wait_send())
        pl.when(z > 0)(lambda k=k: hop(k, z, 1).wait_send())
        for d in range(1, n):
            pl.when((z >= d) & (z < n - 1))(
                lambda k=k, d=d: hop(k, jnp.maximum(z - d, 0), 0).wait_send())
            pl.when((z + d < n) & (z > 0))(
                lambda k=k, d=d: hop(k, jnp.minimum(z + d, n - 1), 1).wait_send())
    for cp in sends:
        cp.wait_send()


def body(
    normed_hidden_rows,
    base_query,
    base_key_value,
    key_value_cache,
    cached_length_per_request,
    request_page_table,
    planned_request_rows,
    request_adapters,
    query_key_value_down_maps,
    query_up_maps,
    key_value_up_maps,
    output_down_maps,
    output_up_maps,
    output_weight_matrix,
):
    n = lax.axis_size("adapter")
    nh = lax.axis_size("head")
    ng = lax.axis_size("groups")
    rows, feats = normed_hidden_rows.shape
    total = planned_request_rows.shape[0]
    na, _, rank = output_down_maps.shape
    slot = max(16, 2 * rows // n)
    cells = n * slot
    qw = base_query.shape[1]
    kvw = base_key_value.shape[2]
    kvl = kvw // HD
    half = qw // kvl
    dw = half + 2 * HD
    cols = output_weight_matrix.shape[1]
    cw = min(512, cols)
    nc = cols // cw
    pages, _, page_len, _ = key_value_cache.shape
    ct = CHUNK_PAGES * page_len
    gr = QH // KVH * rows
    out_rows = total // nh
    rl = rank // nh
    vm = pl.BlockSpec(memory_space=pltpu.VMEM)
    hb = pl.BlockSpec(memory_space=pl.ANY)
    dma = pltpu.SemaphoreType.DMA
    ups = output_up_maps.reshape(na * output_up_maps.shape[1], -1)
    downs = jnp.swapaxes(query_key_value_down_maps, 1, 2).reshape(na * 3 * rank, feats)
    odowns = jnp.swapaxes(output_down_maps, 1, 2).reshape(na * rank, qw)
    qups = query_up_maps.reshape(na * rank, qw)
    return pl.pallas_call(
        functools.partial(kernel, (n, nh, rows, slot, na, rank)),
        out_shape=jax.ShapeDtypeStruct((out_rows, cols), BF),
        in_specs=[vm] * 7 + [hb] * 7,
        out_specs=vm,
        scratch_shapes=[
            pltpu.VMEM(key_value_cache.shape, BF),
            pltpu.VMEM(downs.shape, BF),
            pltpu.VMEM(qups.shape, BF),
            pltpu.VMEM(key_value_up_maps.shape, BF),
            pltpu.VMEM(odowns.shape, BF),
            pltpu.VMEM(output_weight_matrix.shape, BF),
            pltpu.VMEM((n, slot, feats), BF),
            pltpu.VMEM((n, slot, feats), BF),
            pltpu.VMEM((cells, 3 * rank), F32),
            pltpu.VMEM((nh, cells, 3 * rank), F32),
            pltpu.VMEM((kvl, n, slot, dw), BF),
            pltpu.VMEM((kvl, n, slot, dw), BF),
            pltpu.VMEM((n, ups.shape[0], cols), BF),
            pltpu.VMEM((pages // CHUNK_PAGES, rows, ct), F32),
            pltpu.VMEM((pages // CHUNK_PAGES, gr, ct), F32),
            pltpu.VMEM((kvl, n, rows, half), BF),
            pltpu.VMEM((nc, total, cw), F32),
            pltpu.VMEM((nh, rl, total), F32),
            pltpu.VMEM((n * nh, rl, total), F32),
            pltpu.VMEM((nc, nh // 2, out_rows, cw), BF),
            pltpu.VMEM((nc, nh // 2, out_rows, cw), BF),
            pltpu.VMEM((nc, nh // 2, out_rows, cw), BF),
            pltpu.VMEM((nc, nh // 2, out_rows, cw), BF),
            dma((7,)),
            dma((n,)), dma((n,)),
            dma((nh,)), dma((nh,)),
            dma((kvl, n)), dma((kvl, n)),
            dma((n,)), dma((n,)),
            dma((ng, n)), dma((ng, n)),
            dma((2, kvl, n)), dma((kvl, n)),
            dma((n * nh,)), dma((n * nh,)),
            dma((nc,)), dma((nc,)),
            dma((nc, nh // 2)), dma((nc, nh // 2)),
        ],
        compiler_params=pltpu.CompilerParams(
            collective_id=0, has_side_effects=True, vmem_limit_bytes=58 * 1024 * 1024),
    )(
        normed_hidden_rows, base_query, base_key_value,
        cached_length_per_request.reshape(1, rows), request_page_table,
        planned_request_rows.reshape(1, total), request_adapters.reshape(1, total),
        key_value_cache, downs, qups, key_value_up_maps,
        odowns, ups, output_weight_matrix,
    )


def solution(mesh):
    return jax.shard_map(
        body,
        mesh=mesh,
        in_specs=(
            P(("groups", "adapter"), "head"),
            P(("groups", "adapter"), "head"),
            P(("groups", "adapter"), None, "head"),
            P(("groups", "adapter"), None, None, "head"),
            P(("groups", "adapter")),
            P(("groups", "adapter"), None),
            P("groups"),
            P("groups"),
            P("adapter", "head", None),
            P("adapter", None, "head"),
            P("adapter", None, None, "head"),
            P("adapter", "head", None),
            P("adapter", "head", None),
            P("head", "adapter"),
        ),
        out_specs=P(("groups", "head"), "adapter"),
        check_vma=False,
    )
```
